256 devices in a mesh: dom: 32 (over z, x), band: 8 (over y, core).
Axes of the slice: x: 4, y: 4, z: 8, core: 2. Of those that a mesh axis runs over, the one named last changes fastest.
Arguments:
- orbitals: bfloat16 [128, 256, 32, 128], P('band', 'dom'), may hold values from -6 to 6
- potential: float32 [256, 32, 128], P('dom'), may hold values from -6 to 6
- coupling: float32 [8, 8], replicated, may hold values from -2 to 2
- projectors: bfloat16 [8192, 512], P('dom'), may hold values from -1.1953125 to 1.1953125
- slot_atom: int32 [8192], P('dom'), may hold values from 0 to 2047, as said below
- slot_domain_block: int32 [8192], P('dom'), may hold values from 0 to 511
- slot_count: int32 [32], P('dom'), may hold values from 64 to 256
Outputs:
- applied: bfloat16 [128, 256, 32, 128], P('band', 'dom')
- subspace: float32 [128, 128], P('band')
The draws below stay inside these ranges and needn't reach their ends.
Inputs may be any that keep to these rules, and one draw needn't show every extreme that they name: `slot_atom`: every slot of domain d names an atom whose owner, atom // 64, is d - 1, d or d + 1, counted cyclically over the 32 domains.
All inputs are finite; a program needn't handle non-finite values.
Results may differ from the reference program's by a relative error of at most 0.0038.
Values may be sent and summed in bfloat16 or wider, within the bound.
A program may use at most 128 MiB of HBM per device.

```python
import jax
import jax.numpy as jnp
from jax import lax

ORBS = 128
ATOM_PROJECTORS = 8
BLOCK_POINTS = 64
DOMAIN_PLANES = 8
CELLS_SECOND = 32
CELLS_THIRD = 128
ATOMS_PER_DOMAIN = 64
DOMAIN_SLOTS = 256
DOMAINS = 32
ATOMS = 2048
TOTAL_SLOTS = 8192
NX = 256


def plane_amplitude(lowest, ratio):
    plane_index = jnp.arange(NX, dtype=jnp.int32) % DOMAIN_PLANES
    fraction = plane_index.astype(jnp.float32) / float(DOMAIN_PLANES - 1)
    return (lowest * jnp.exp(fraction * jnp.log(ratio))).reshape(1, NX, 1, 1)


def draw_orbitals(key, part):
    key = jax.random.fold_in(key, 11)
    leading_key, trailing_key, third_key = jax.random.split(key, 3)
    own_noise = jax.random.normal(leading_key, (ORBS, NX, CELLS_SECOND, CELLS_THIRD), jnp.float32)
    shared = jax.random.normal(trailing_key, (NX, CELLS_SECOND, CELLS_THIRD), jnp.float32)
    weights = jax.random.uniform(third_key, (ORBS, 1, 1, 1), jnp.float32, -1.0, 1.0)
    amplitude = plane_amplitude(0.5, 4.0)
    values = amplitude * (0.8 * own_noise + weights * shared[None])
    return jnp.clip(values, -6.0, 6.0).astype(jnp.bfloat16)


def draw_slot_atom(key, part):
    key = jax.random.fold_in(key, 23)
    leading_key, trailing_key = jax.random.split(key)
    home_domain = jnp.arange(TOTAL_SLOTS, dtype=jnp.int32) // DOMAIN_SLOTS
    lane_position_index = jnp.arange(TOTAL_SLOTS, dtype=jnp.int32) % DOMAIN_SLOTS
    reach_displacement = jax.random.randint(leading_key, (TOTAL_SLOTS,), 0, 3, dtype=jnp.int32) - 1
    member_position_index = jax.random.randint(trailing_key, (TOTAL_SLOTS,), 0, ATOMS_PER_DOMAIN, dtype=jnp.int32)
    owner_dom = (home_domain + reach_displacement + DOMAINS) % DOMAINS
    atom_ids = owner_dom * ATOMS_PER_DOMAIN + member_position_index
    atom_ids = jnp.where(lane_position_index == 0, home_domain * ATOMS_PER_DOMAIN + ATOMS_PER_DOMAIN - 1, atom_ids)
    atom_ids = jnp.where(lane_position_index == 1, home_domain * ATOMS_PER_DOMAIN, atom_ids)
    return atom_ids.astype(jnp.int32)


def draw_slot_count(key, part):
    key = jax.random.fold_in(key, 37)
    leading_key, trailing_key = jax.random.split(key)
    counts = jax.random.randint(leading_key, (DOMAINS,), DOMAIN_SLOTS // 4, DOMAIN_SLOTS + 1, dtype=jnp.int32)
    busiest = jax.random.randint(trailing_key, (), 0, DOMAINS, dtype=jnp.int32)
    domain_index = jnp.arange(DOMAINS, dtype=jnp.int32)
    counts = jnp.where(domain_index == busiest, DOMAIN_SLOTS, counts)
    counts = jnp.where(domain_index == (busiest + 1) % DOMAINS, DOMAIN_SLOTS // 4, counts)
    return counts.astype(jnp.int32)


def place_ends(drawn, rng, least, high):
    longest = drawn.shape.index(max(drawn.shape))
    spots = []
    for shift in (0, 1):
        where = [jax.random.randint(jax.random.fold_in(rng, axis), (), 0, length) for axis, length in enumerate(drawn.shape)]
        where[longest] = (where[longest] + shift) % drawn.shape[longest]
        spots.append(tuple(where))
    return drawn.at[spots[0]].set(least).at[spots[1]].set(high)


def steps_of(rng, dims, shards, low, largest):
    def one(position, blocks):
        heights = jax.random.uniform(jax.random.fold_in(jax.random.fold_in(rng, 6), position), (blocks,), jnp.float32, low / len(shards), largest / len(shards))
        return jnp.repeat(jnp.exp(heights), dims[position] // blocks).reshape((-1,) + (1,) * (len(dims) - position - 1))

    level = one(*shards[0])
    for cut in shards[1:]:
        level = level * one(*cut)
    return level


def scatter_about(key, shape, deviation, bound, cuts=(), kind=jnp.bfloat16):
    values = jax.random.normal(key, shape, jnp.float32) * deviation
    if len(cuts) > 0:
        values = steps_of(key, shape, cuts, -0.22, 0.18) * values
    return jnp.clip(values, min=-bound, max=bound).astype(kind)


def setup_inputs(seed: int = 0) -> dict:
    keys = jax.random.split(jax.random.key(seed), 8)
    return {
        "orbitals": draw_orbitals(jax.random.fold_in(keys[7], 71), 0),
        "potential": scatter_about(keys[1], (NX, CELLS_SECOND, CELLS_THIRD), 1.0, 6.0, ((0, 32),), jnp.float32),
        "coupling": scatter_about(keys[2], (ATOM_PROJECTORS, ATOM_PROJECTORS), ATOM_PROJECTORS ** -0.5, 2.0, (), jnp.float32),
        "projectors": scatter_about(keys[3], (TOTAL_SLOTS, ATOM_PROJECTORS * BLOCK_POINTS), 0.2, 1.1953125, ((0, 32),)),
        "slot_atom": draw_slot_atom(jax.random.fold_in(keys[7], 71), 0),
        "slot_domain_block": place_ends(jax.random.randint(keys[5], (TOTAL_SLOTS,), 0, DOMAIN_PLANES * CELLS_SECOND * CELLS_THIRD // BLOCK_POINTS), jax.random.fold_in(keys[5], 1), 0, (DOMAIN_PLANES * CELLS_SECOND * CELLS_THIRD // BLOCK_POINTS) - 1).astype(jnp.int32),
        "slot_count": draw_slot_count(jax.random.fold_in(keys[7], 71), 0),
    }


STENCIL = (-205.0 / 72.0, 8.0 / 5.0, -1.0 / 5.0, 8.0 / 315.0, -1.0 / 560.0)


def laplacian(values):
    summed = 3.0 * STENCIL[0] * values
    for dimension in range(3):
        for offset in range(1, 5):
            summed = summed + STENCIL[offset] * (jnp.roll(values, offset, dimension) + jnp.roll(values, -offset, dimension))
    return summed


def reference(orbitals, potential, coupling, projectors, slot_atom, slot_domain_block, slot_count):
    points = DOMAIN_PLANES * CELLS_SECOND * CELLS_THIRD
    blocks_dom = points // BLOCK_POINTS
    lane_position_index = jnp.arange(TOTAL_SLOTS, dtype=jnp.int32) % DOMAIN_SLOTS
    owning_domains = jnp.arange(TOTAL_SLOTS, dtype=jnp.int32) // DOMAIN_SLOTS
    live_mask = (lane_position_index < slot_count[owning_domains]).astype(jnp.float32)
    block_rows = (owning_domains * blocks_dom + slot_domain_block).astype(jnp.int32)
    reshaped_array = projectors.astype(jnp.float32).reshape(TOTAL_SLOTS, ATOM_PROJECTORS, BLOCK_POINTS)

    def apply_one(orbital):
        values = orbital.astype(jnp.float32)
        local_part = -0.5 * laplacian(values) + potential * values
        flat_orbs = orbital.reshape(DOMAINS * blocks_dom, BLOCK_POINTS)
        picked = flat_orbs[block_rows].astype(jnp.float32)
        slot_coef = jnp.einsum("spk,sk->sp", reshaped_array, picked) * live_mask[:, None]
        coefficients = jax.ops.segment_sum(slot_coef, slot_atom, num_segments=ATOMS)
        coupled = jnp.dot(coefficients, coupling.T, precision=lax.Precision.HIGHEST).astype(jnp.bfloat16)
        spread = coupled[slot_atom].astype(jnp.float32)
        contrib = jnp.einsum("spk,sp->sk", reshaped_array, spread) * live_mask[:, None]
        projected = jax.ops.segment_sum(contrib, block_rows, num_segments=DOMAINS * blocks_dom)
        return (local_part + projected.reshape(NX, CELLS_SECOND, CELLS_THIRD)).astype(jnp.bfloat16)

    applied = lax.map(apply_one, orbitals)
    gram_matrix = jnp.dot(orbitals.reshape(ORBS, NX * CELLS_SECOND * CELLS_THIRD), applied.reshape(ORBS, NX * CELLS_SECOND * CELLS_THIRD).T, preferred_element_type=jnp.float32)
    gram_matrix = gram_matrix / float(NX * CELLS_SECOND * CELLS_THIRD)
    return applied, gram_matrix
```

```python
import functools

import jax
import jax.numpy as jnp
from jax import lax
from jax.experimental import pallas as pl
from jax.experimental.pallas import tpu as pltpu
from jax.sharding import PartitionSpec as P

MESH = pl.DeviceIdType.MESH
F32 = jnp.float32
BF16 = jnp.bfloat16
STENCIL = (-205.0 / 72.0, 8.0 / 5.0, -1.0 / 5.0, 8.0 / 315.0, -1.0 / 560.0)
ALONG_X = 4
NN = (((1,), (0,)), ((), ()))
NT = (((1,), (1,)), ((), ()))
ORDER = (3, 4, 2, 5, 1, 6, 0, 7)


def mm(a, b, dims=NN):
    return lax.dot_general(a, b, dims, preferred_element_type=F32)


def iota(shape, dim):
    return lax.broadcasted_iota(jnp.int32, shape, dim)


def one(mask):
    return jnp.where(mask, 1.0, 0.0).astype(BF16)


def split(value):
    high = value.astype(BF16)
    return high, (value - high.astype(F32)).astype(BF16)


def plane_matrix():
    r, c = iota((256, 256), 0), iota((256, 256), 1)
    same_plane, same_row = (r >> 5) == (c >> 5), (r & 31) == (c & 31)
    apart, turn = jnp.abs((r >> 5) - (c >> 5)), ((r & 31) - (c & 31)) & 31
    value = jnp.where(r == c, -1.5 * STENCIL[0], 0.0)
    for k in range(1, 5):
        value = jnp.where(same_plane & ((turn == k) | (turn == 32 - k)), -0.5 * STENCIL[k], value)
        value = jnp.where(same_row & (apart == k), -0.5 * STENCIL[k], value)
    return value


def lane_matrix():
    turn = (iota((128, 128), 0) - iota((128, 128), 1)) & 127
    value = jnp.zeros((128, 128), F32)
    for k in range(1, 5):
        value = jnp.where((turn == k) | (turn == 128 - k), -0.5 * STENCIL[k], value)
    return value


def kernel(
    domains, bands,
    v, pot, coupling, proj, atom, block, count,
    out, gram_out,
    vt, va, wt, wa, low, high, acc, gt, gm, hm, at, pt, cf, sp, q, rq, pm, lm, zm, gram, rb, rx, rz,
    barrier_unused, v_send, v_recv, w_send, w_recv, h_send, h_recv, q_send, q_recv, s_send, s_recv, own_sem,
):
    dom, band = lax.axis_index("dom"), lax.axis_index("band")
    x, z = lax.rem(dom, ALONG_X), dom // ALONG_X
    rows_z = domains // ALONG_X

    def dom_at(step):
        return {"dom": lax.rem(dom + step + domains, domains)}

    def band_at(step):
        return {"band": lax.rem(band + step, bands)}

    def x_at(step):
        return {"dom": z * ALONG_X + lax.rem(x + step, ALONG_X)}

    def z_at(step):
        return {"dom": lax.rem(z + step, rows_z) * ALONG_X + x}

    peers = [dom_at(step) for step in (1, -1, 2, -2)]
    peers += [band_at(step) for step in range(1, bands)]
    peers += [x_at(step) for step in range(1, ALONG_X)]
    peers += [z_at(step) for step in range(1, rows_z)]
    barrier = pltpu.get_barrier_semaphore()
    for peer in peers:
        pl.semaphore_signal(barrier, inc=1, device_id=peer, device_id_type=MESH)

    def send(src, dst, send_sem, recv_sem, peer):
        copy = pltpu.make_async_remote_copy(
            src_ref=src, dst_ref=dst, send_sem=send_sem, recv_sem=recv_sem, device_id=peer, device_id_type=MESH
        )
        copy.start()
        return copy

    r, c = iota((256, 256), 0), iota((256, 256), 1)
    pm[...] = one(((r & 15) == (c >> 4)) & ((r >> 4) == (c & 15)))

    def turned(piece, target, half, position):
        tiles = mm(pm[...], piece.reshape(256, 128)).astype(BF16).reshape(16, 16, 128)
        for row in range(16):
            target[4 * half + row // 4, :, pl.ds((position * 4 + row % 4) * 128, 128)] = tiles[row]

    for position, plane in enumerate(ORDER):
        for half in range(2):
            turned(v[:, plane, 16 * half : 16 * half + 16, :], vt, half, position)

    pl.semaphore_wait(barrier, len(peers))

    v_copies = []
    for step in range(1, bands):
        peer = band_at(step)
        v_copies.append(send(vt.at[peer["band"]], va.at[band], v_send.at[step - 1], v_recv.at[step - 1], peer))
    h_copies = []
    for k in range(1, 5):
        h_copies.append((
            send(v.at[:, 8 - k], low.at[4 - k], h_send.at[0, k - 1], h_recv.at[0, k - 1], dom_at(1)),
            send(v.at[:, k - 1], high.at[k - 1], h_send.at[1, k - 1], h_recv.at[1, k - 1], dom_at(-1)),
        ))
    own_v = pltpu.make_async_copy(vt.at[band], va.at[band], own_sem.at[0])
    own_v.start()

    half_of = block[...] & 1
    live = iota((1, 256), 1) < count[0]
    gt[...] = one((r == (block[...] >> 1)) & live)
    eye = one(r == c)
    gm[...] = mm(eye, gt[...], NT).astype(BF16)
    hm[...] = mm(eye, one((iota((128, 256), 0) >> 6) == half_of), NT)
    window = (((atom[...] >> 6) - dom + 1 + domains) & (domains - 1)) * 64 + (atom[...] & 63)
    at[...] = one(iota((192, 256), 0) == window)
    small_eye = one(iota((128, 128), 0) == iota((128, 128), 1))
    for pair in range(4):
        pt[2 * pair : 2 * pair + 2] = mm(small_eye, proj[:, 128 * pair : 128 * pair + 128], NT).reshape(2, 64, 256)
    fold = one((iota((64, 128), 1) & 63) == iota((64, 128), 0))

    @pl.loop(0, 16)
    def _(o):
        picked = (mm(gm[...], v[o].reshape(256, 128)) * hm[...]).astype(BF16)
        points = mm(fold, picked, NT)
        for p in range(8):
            cf[p, pl.ds(o, 1), :] = jnp.sum(points * pt[p], axis=0, keepdims=True)

    rest = cf[...].reshape(128, 256)
    total = jnp.zeros((192, 128), F32)
    for _ in range(3):
        part = rest.astype(BF16)
        rest = rest - part.astype(F32)
        total = total + mm(at[...], part, NT)
    q[...] = total.reshape(3, 64, 128)
    q_copies = [
        send(q.at[pl.ds(1, 2)], rq.at[pl.ds(1, 2)], q_send.at[0], q_recv.at[0], dom_at(1)),
        send(q.at[pl.ds(0, 2)], rq.at[pl.ds(3, 2)], q_send.at[1], q_recv.at[1], dom_at(-1)),
        send(q.at[2], rq.at[0], q_send.at[2], q_recv.at[2], dom_at(2)),
        send(q.at[0], rq.at[5], q_send.at[3], q_recv.at[3], dom_at(-2)),
    ]

    lm[0:256], lm[256:512] = split(plane_matrix())
    zm[:, 0:128], zm[:, 128:256] = split(lane_matrix())

    @pl.loop(0, 16)
    def _(o):
        values = v[o].reshape(256, 128)
        both = mm(lm[...], values)
        lanes = mm(values, zm[...])
        summed = both[0:256] + both[256:512] + lanes[:, 0:128] + lanes[:, 128:256]
        acc[o] = (summed + pot[...].reshape(256, 128) * values.astype(F32)).reshape(8, 32, 128)

    rows = []
    for p in range(8):
        line = jnp.zeros((16, 128), F32)
        for j in range(8):
            line = jnp.where((iota((16, 128), 1) >> 4) == j, coupling[p, j], line)
        rows.append(jnp.where((iota((16, 128), 1) & 15) == iota((16, 128), 0), line, 0.0))
    mixing = jnp.concatenate(rows, axis=0)

    for copy in q_copies:
        copy.wait_recv()
    owned = jnp.concatenate([rq[0] + rq[1] + q[0], rq[2] + q[1] + rq[3], q[2] + rq[4] + rq[5]], axis=0)
    coupled = lax.dot_general(mixing, owned, NT, precision=lax.Precision.HIGHEST, preferred_element_type=F32)
    sp[...] = mm(coupled.astype(BF16), at[...]).reshape(8, 16, 256)

    @pl.loop(0, 16)
    def _(o):
        added = pt[0] * sp[0, pl.ds(o, 1), :]
        for p in range(1, 8):
            added = added + pt[p] * sp[p, pl.ds(o, 1), :]
        placed = jnp.concatenate([jnp.where(half_of == 0, added, 0.0), jnp.where(half_of == 1, added, 0.0)], axis=0)
        first, second = split(placed)
        acc[o] = acc[o] + (mm(gt[...], first, NT) + mm(gt[...], second, NT)).reshape(8, 32, 128)

    w_copies = []
    for k in range(1, 5):
        for copy in h_copies[k - 1]:
            copy.wait_recv()
        for side in range(2):
            plane = 3 + k if side else 4 - k
            for half in range(2):
                span = slice(16 * half, 16 * half + 16)
                value = acc[:, plane, span, :]
                for near in range(k):
                    halo = high[near, :, span, :] if side else low[3 - near, :, span, :]
                    reach = 8 + near - plane if side else plane + 1 + near
                    value = value - 0.5 * STENCIL[reach] * halo.astype(F32)
                value = value.astype(BF16)
                out[:, plane, span, :] = value
                turned(value, wt, half, 2 * (k - 1) + side)
        span = pl.ds((k - 1) * 1024, 1024)
        step_copies = []
        for step in range(1, bands):
            peer = band_at(step)
            step_copies.append(send(
                wt.at[peer["band"], :, span], wa.at[band, :, span],
                w_send.at[k - 1, step - 1], w_recv.at[k - 1, step - 1], peer,
            ))
        w_copies.append(step_copies)
        wa[band, :, span] = wt[band, :, span]

    for copy in v_copies:
        copy.wait_recv()
    own_v.wait()
    for k in range(1, 5):
        for copy in w_copies[k - 1]:
            copy.wait_recv()
        span = slice((k - 1) * 1024, k * 1024)
        part = mm(va[:, :, span].reshape(128, 1024), wa[:, :, span].reshape(128, 1024), NT)
        gram[...] = part if k == 1 else gram[...] + part

    s_copies = []
    for step in range(1, bands):
        peer = band_at(step)
        s_copies.append(send(
            gram.at[pl.ds(pl.multiple_of(peer["band"] * 16, 16), 16)], rb.at[band],
            s_send.at[step - 1], s_recv.at[step - 1], peer,
        ))
    rb[band] = gram[pl.ds(pl.multiple_of(band * 16, 16), 16)]
    for copy in s_copies:
        copy.wait_recv()
    rx[x] = jnp.sum(rb[...], axis=0)
    x_copies = [
        send(rx.at[x], rx.at[x], s_send.at[6 + step], s_recv.at[6 + step], x_at(step)) for step in range(1, ALONG_X)
    ]
    for copy in x_copies:
        copy.wait_recv()
    rz[z] = jnp.sum(rx[...], axis=0)
    z_copies = [
        send(rz.at[z], rz.at[z], s_send.at[9 + step], s_recv.at[9 + step], z_at(step)) for step in range(1, rows_z)
    ]
    for copy in z_copies:
        copy.wait_recv()
    gram_out[...] = jnp.sum(rz[...], axis=0) * (1.0 / (domains * 32768))

    for copy in v_copies + q_copies + s_copies + x_copies + z_copies:
        copy.wait_send()
    for copies in h_copies + w_copies:
        for copy in copies:
            copy.wait_send()


def local(domains, bands, orbitals, potential, coupling, projectors, slot_atom, slot_domain_block, slot_count):
    vmem = pl.BlockSpec(memory_space=pltpu.VMEM)
    smem = pl.BlockSpec(memory_space=pltpu.SMEM)
    shift = domains // ALONG_X + ALONG_X + bands - 3
    return pl.pallas_call(
        functools.partial(kernel, domains, bands),
        out_shape=(
            jax.ShapeDtypeStruct((16, 8, 32, 128), BF16),
            jax.ShapeDtypeStruct((16, 128), F32),
        ),
        in_specs=[vmem, vmem, smem, vmem, vmem, vmem, smem],
        out_specs=(vmem, vmem),
        scratch_shapes=[
            pltpu.VMEM((8, 16, 4096), BF16),
            pltpu.VMEM((8, 16, 4096), BF16),
            pltpu.VMEM((8, 16, 4096), BF16),
            pltpu.VMEM((8, 16, 4096), BF16),
            pltpu.VMEM((4, 16, 32, 128), BF16),
            pltpu.VMEM((4, 16, 32, 128), BF16),
            pltpu.VMEM((16, 8, 32, 128), F32),
            pltpu.VMEM((256, 256), BF16),
            pltpu.VMEM((256, 256), BF16),
            pltpu.VMEM((256, 128), F32),
            pltpu.VMEM((192, 256), BF16),
            pltpu.VMEM((8, 64, 256), F32),
            pltpu.VMEM((8, 16, 256), F32),
            pltpu.VMEM((8, 16, 256), F32),
            pltpu.VMEM((3, 64, 128), F32),
            pltpu.VMEM((6, 64, 128), F32),
            pltpu.VMEM((256, 256), BF16),
            pltpu.VMEM((512, 256), BF16),
            pltpu.VMEM((128, 256), BF16),
            pltpu.VMEM((128, 128), F32),
            pltpu.VMEM((8, 16, 128), F32),
            pltpu.VMEM((ALONG_X, 16, 128), F32),
            pltpu.VMEM((domains // ALONG_X, 16, 128), F32),
            pltpu.SemaphoreType.DMA,
            pltpu.SemaphoreType.DMA((7,)),
            pltpu.SemaphoreType.DMA((7,)),
            pltpu.SemaphoreType.DMA((4, 7)),
            pltpu.SemaphoreType.DMA((4, 7)),
            pltpu.SemaphoreType.DMA((2, 4)),
            pltpu.SemaphoreType.DMA((2, 4)),
            pltpu.SemaphoreType.DMA((4,)),
            pltpu.SemaphoreType.DMA((4,)),
            pltpu.SemaphoreType.DMA((shift,)),
            pltpu.SemaphoreType.DMA((shift,)),
            pltpu.SemaphoreType.DMA((1,)),
        ],
        compiler_params=pltpu.CompilerParams(
            collective_id=0, has_side_effects=True, vmem_limit_bytes=40 * 1024 * 1024
        ),
    )(
        orbitals, potential, coupling, projectors,
        slot_atom.reshape(1, -1), slot_domain_block.reshape(1, -1), slot_count,
    )


def solution(mesh):
    return jax.shard_map(
        functools.partial(local, mesh.shape["dom"], mesh.shape["band"]),
        mesh=mesh,
        in_specs=(
            P("band", "dom", None, None),
            P("dom", None, None),
            P(),
            P("dom", None),
            P("dom"),
            P("dom"),
            P("dom"),
        ),
        out_specs=(P("band", "dom", None, None), P("band", None)),
        check_vma=False,
    )
```

```python
import functools

import jax
import jax.numpy as jnp
from jax import lax
from jax.experimental import pallas as pl
from jax.experimental.pallas import tpu as pltpu
from jax.sharding import PartitionSpec as P

MESH = pl.DeviceIdType.MESH
F32 = jnp.float32
BF16 = jnp.bfloat16
STENCIL = (-205.0 / 72.0, 8.0 / 5.0, -1.0 / 5.0, 8.0 / 315.0, -1.0 / 560.0)
NN = (((1,), (0,)), ((), ()))
NT = (((1,), (1,)), ((), ()))
LANES = 16
REACH = 4


def mm(a, b, dims=NN):
    return lax.dot_general(a, b, dims, preferred_element_type=F32)


def iota(shape, dim):
    return lax.broadcasted_iota(jnp.int32, shape, dim)


def one(mask):
    return jnp.where(mask, 1.0, 0.0).astype(BF16)


def split(value):
    high = value.astype(BF16)
    return high, (value - high.astype(F32)).astype(BF16)


def plane_matrix():
    r, c = iota((256, 256), 0), iota((256, 256), 1)
    same_plane, same_row = (r >> 5) == (c >> 5), (r & 31) == (c & 31)
    apart, turn = jnp.abs((r >> 5) - (c >> 5)), ((r & 31) - (c & 31)) & 31
    value = jnp.where(r == c, -1.5 * STENCIL[0], 0.0)
    for k in range(1, 5):
        value = jnp.where(same_plane & ((turn == k) | (turn == 32 - k)), -0.5 * STENCIL[k], value)
        value = jnp.where(same_row & (apart == k), -0.5 * STENCIL[k], value)
    return value


def lane_matrix():
    turn = (iota((128, 128), 0) - iota((128, 128), 1)) & 127
    value = jnp.zeros((128, 128), F32)
    for k in range(1, 5):
        value = jnp.where((turn == k) | (turn == 128 - k), -0.5 * STENCIL[k], value)
    return value


def boundary_matrix(parity):
    r, c = iota((128, 128), 0), iota((128, 128), 1)
    apart = ((c >> 5) - (r >> 5)) * (1 - 2 * parity)
    value = jnp.zeros((128, 128), F32)
    for k in range(1, 5):
        value = jnp.where(((r & 31) == (c & 31)) & (apart == 4 - k), -0.5 * STENCIL[k], value)
    return value


def kernel(
    domains, bands,
    v_in, pot_in, coupling, proj_in, atom_in, block_in, count,
    out, gram_out,
    v, pot, proj, atom, block, tv, vt, va, hb, low, high, acc, gt, at, pt, cf, sp, q, rq, pm, lm, zm, mb, pott, p3, ra,
    gram, rb, rd,
    in_sem, a_send, a_recv, b_send, b_recv, f_send, f_recv, h_send, h_recv, q_send, q_recv, n_send, n_recv, s_send, s_recv, own_sem,
):
    dom, band = lax.axis_index("dom"), lax.axis_index("band")

    def dom_at(step):
        return {"dom": lax.rem(dom + step + domains, domains)}

    def band_at(step):
        return {"band": lax.rem(band + step, bands)}

    loads = [
        pltpu.make_async_copy(src, dst, in_sem.at[place])
        for place, (src, dst) in enumerate(
            ((v_in, v), (block_in, block), (proj_in, proj), (atom_in, atom), (pot_in, pot))
        )
    ]
    for load in loads:
        load.start()

    peers = [band_at(step) for step in range(1, bands)] + [dom_at(step) for step in range(1, domains)]
    barrier = pltpu.get_barrier_semaphore()
    for peer in peers:
        pl.semaphore_signal(barrier, inc=1, device_id=peer, device_id_type=MESH)

    def send(src, dst, send_sem, recv_sem, peer):
        copy = pltpu.make_async_remote_copy(
            src_ref=src, dst_ref=dst, send_sem=send_sem, recv_sem=recv_sem, device_id=peer, device_id_type=MESH
        )
        copy.start()
        return copy

    r, c = iota((256, 256), 0), iota((256, 256), 1)
    loads[0].wait()
    pm[...] = one(((r & 15) == (c >> 4)) & ((r >> 4) == (c & 15)))

    small_eye = one(iota((128, 128), 0) == iota((128, 128), 1))

    @pl.loop(0, 16, step=4)
    def _(first):
        for i in range(4):
            tv[first + i] = mm(small_eye, v[first + i].reshape(256, 128), NT).astype(BF16)

    for share in range(8):
        span = slice(LANES * share, LANES * share + LANES)
        tiles = mm(pm[...], tv[:, span, :].reshape(256, 256)).astype(BF16).reshape(LANES, 16, 256)
        vt[0, span] = tiles[:, :, 0:128]
        vt[1, span] = tiles[:, :, 128:256]
    vt[:, 128 : 128 + REACH] = vt[:, 0:REACH]

    pl.semaphore_wait(barrier, len(peers))

    parity = lax.rem(band, 2)
    a_copies, b_copies = [], []
    for step in range(1, bands):
        peer = band_at(step)
        other, side = peer["band"], lax.rem(peer["band"], 2)
        a_copies.append(send(
            vt.at[side, pl.ds(LANES * other, LANES)], va.at[band, side, pl.ds(0, LANES)],
            a_send.at[step - 1], a_recv.at[step - 1], peer,
        ))
    own = pltpu.make_async_copy(vt.at[:, pl.ds(LANES * band, LANES + REACH)], va.at[band], own_sem.at[0])
    own.start()

    def send_halos(k):
        return (
            send(v.at[:, 8 - k], low.at[4 - k], h_send.at[0, k - 1], h_recv.at[0, k - 1], dom_at(1)),
            send(v.at[:, k - 1], high.at[k - 1], h_send.at[1, k - 1], h_recv.at[1, k - 1], dom_at(-1)),
        )

    h_copies = [send_halos(1), send_halos(2)]
    for step in range(1, bands):
        peer = band_at(step)
        other, side = peer["band"], lax.rem(peer["band"], 2)
        b_copies.append(send(
            vt.at[1 - side, pl.ds(LANES * other, LANES + REACH)], va.at[band, 1 - side],
            b_send.at[0, step - 1], b_recv.at[0, step - 1], peer,
        ))
        b_copies.append(send(
            vt.at[side, pl.ds(LANES * other + LANES, REACH)], va.at[band, side, pl.ds(LANES, REACH)],
            b_send.at[1, step - 1], b_recv.at[1, step - 1], peer,
        ))

    onward = dom_at(2 * parity - 1)

    def forward(source, place):
        return send(va.at[source, parity, pl.ds(0, LANES)], hb.at[source], f_send.at[place], f_recv.at[place], onward)

    for load in loads[1:]:
        load.wait()
    half_of = block[...] & 1
    live = iota((1, 256), 1) < count[0]
    gt[...] = one((r == (block[...] >> 1)) & live)
    window = (((atom[...] >> 6) - dom + 1 + domains) & (domains - 1)) * 64 + (atom[...] & 63)
    at[...] = one(iota((192, 256), 0) == window)
    for pair in range(4):
        pt[2 * pair : 2 * pair + 2] = mm(small_eye, proj[:, 128 * pair : 128 * pair + 128], NT).reshape(2, 64, 256)

    @pl.loop(0, 16, step=4)
    def _(first):
        picked = mm(tv[pl.ds(first, 4)].reshape(512, 256), gt[...])
        for i in range(4):
            points = jnp.where(half_of == 0, picked[128 * i : 128 * i + 64], picked[128 * i + 64 : 128 * i + 128])
            for p in range(8):
                cf[p, pl.ds(first + i, 1), :] = jnp.sum(points * pt[p], axis=0, keepdims=True)

    rest = cf[...].reshape(128, 256)
    total = jnp.zeros((192, 128), F32)
    for _ in range(3):
        part = rest.astype(BF16)
        rest = rest - part.astype(F32)
        total = total + mm(at[...], part, NT)
    q[...] = total.reshape(3, 64, 128)
    q_copies = [
        send(q.at[pl.ds(1, 2)], rq.at[pl.ds(1, 2)], q_send.at[0], q_recv.at[0], dom_at(1)),
        send(q.at[pl.ds(0, 2)], rq.at[pl.ds(3, 2)], q_send.at[1], q_recv.at[1], dom_at(-1)),
        send(q.at[2], rq.at[0], q_send.at[2], q_recv.at[2], dom_at(2)),
        send(q.at[0], rq.at[5], q_send.at[3], q_recv.at[3], dom_at(-2)),
    ]

    lm[:, 0:256], lm[:, 256:512] = split(plane_matrix())
    zm[0:128], zm[128:256] = split(lane_matrix())

    @pl.loop(0, 16, step=2)
    def _(first):
        values = [v[first + i].reshape(256, 128) for i in range(2)]
        wide = jnp.concatenate(values, axis=1)
        summed = mm(lm[...], jnp.concatenate([wide, wide], axis=0))
        for i in range(2):
            lanes = mm(jnp.concatenate([values[i], values[i]], axis=1), zm[...])
            local_part = summed[:, 128 * i : 128 * i + 128] + lanes + pot[...].reshape(256, 128) * values[i].astype(F32)
            acc[first + i] = local_part.reshape(8, 32, 128)

    rows = []
    for p in range(8):
        line = jnp.zeros((16, 128), F32)
        for j in range(8):
            line = jnp.where((iota((16, 128), 1) >> 4) == j, coupling[p, j], line)
        rows.append(jnp.where((iota((16, 128), 1) & 15) == iota((16, 128), 0), line, 0.0))
    mixing = jnp.concatenate(rows, axis=0)

    for copy in q_copies:
        copy.wait_recv()
    owned = jnp.concatenate([rq[0] + rq[1] + q[0], rq[2] + q[1] + rq[3], q[2] + rq[4] + rq[5]], axis=0)
    coupled = lax.dot_general(mixing, owned, NT, precision=lax.Precision.HIGHEST, preferred_element_type=F32)
    own_rows = owned[64:128]
    p3[:, 0:128] = mm(small_eye, jnp.concatenate(split(own_rows), axis=0), NT).astype(BF16)
    p3[:, 128:256] = lax.dot_general(
        mixing, jnp.concatenate([own_rows, own_rows], axis=0), NT, precision=lax.Precision.HIGHEST, preferred_element_type=F32
    ).astype(BF16)
    n_copies = []
    for step in range(1, bands):
        peer = band_at(step)
        n_copies.append(send(
            p3.at[pl.ds(pl.multiple_of(peer["band"] * 16, 16), 16)], ra.at[band],
            n_send.at[step - 1], n_recv.at[step - 1], peer,
        ))
    ra[band] = p3[pl.ds(pl.multiple_of(band * 16, 16), 16), :]
    sp[...] = mm(coupled.astype(BF16), at[...]).reshape(8, 16, 256)

    gt_twice = jnp.concatenate([gt[...], gt[...]], axis=1)

    @pl.loop(0, 16, step=2)
    def _(first):
        placed = []
        for i in range(2):
            added = pt[0] * sp[0, pl.ds(first + i, 1), :]
            for p in range(1, 8):
                added = added + pt[p] * sp[p, pl.ds(first + i, 1), :]
            placed += [jnp.where(half_of == 0, added, 0.0), jnp.where(half_of == 1, added, 0.0)]
        parts = split(jnp.concatenate(placed, axis=0))
        projected = mm(gt_twice, jnp.concatenate(parts, axis=1), NT)
        for i in range(2):
            acc[first + i] = acc[first + i] + projected[:, 128 * i : 128 * i + 128].reshape(8, 32, 128)

    own.wait()
    f_copies = [forward(band, 0)]
    for step, copy in enumerate(a_copies, 1):
        copy.wait_recv()
        f_copies.append(forward(lax.rem(band - step + bands, bands), step))
    h_copies += [send_halos(3), send_halos(4)]

    def finish(k):
        for copy in h_copies[k - 1]:
            copy.wait_recv()
        for side in range(2):
            plane = 3 + k if side else 4 - k
            for half in range(2):
                span = slice(16 * half, 16 * half + 16)
                value = acc[:, plane, span, :]
                for near in range(k):
                    halo = high[near, :, span, :] if side else low[3 - near, :, span, :]
                    reach = 8 + near - plane if side else plane + 1 + near
                    value = value - 0.5 * STENCIL[reach] * halo.astype(F32)
                out[:, plane, span, :] = value.astype(BF16)

    finish(1)
    finish(2)

    pott[...] = pot[...].reshape(256, 128).T
    mb[0:128], mb[128:256] = split(boundary_matrix(parity))
    gram[...] = jnp.zeros_like(gram)
    for copy in b_copies:
        copy.wait_recv()

    @pl.loop(0, LANES, step=4)
    def _(first):
        lanes = [
            jnp.concatenate([va[:, 0, first + i].reshape(128, 128), va[:, 1, first + i].reshape(128, 128)], axis=1)
            for i in range(8)
        ]
        images = []
        for i in range(4):
            weights = pott[pl.ds(LANES * band + first + i, 1), :]
            image = mm(jnp.concatenate([lanes[i], lanes[i]], axis=1), lm[...], NT) + weights * lanes[i].astype(F32)
            images.append(image.astype(BF16))
        rows = [jnp.concatenate(images, axis=1)]
        rows += [jnp.concatenate(lanes[k : k + 4], axis=1) for k in range(1, 5)]
        gram[:, 0:640] += mm(jnp.concatenate(lanes[0:4], axis=1), jnp.concatenate(rows, axis=0), NT)

    for copy in f_copies:
        copy.wait_recv()

    @pl.loop(0, LANES, step=4)
    def _(first):
        near, far = [], []
        for i in range(4):
            near.append(va[:, 1 - parity, first + i].reshape(128, 128))
            across = hb[:, first + i].reshape(128, 128)
            far.append(mm(jnp.concatenate([across, across], axis=1), mb[...]).astype(BF16))
        gram[:, 640:768] += mm(jnp.concatenate(near, axis=1), jnp.concatenate(far, axis=1), NT)

    for copy in n_copies:
        copy.wait_recv()
    once = gram[:, 640:768]
    for k in range(1, 5):
        once = once - 0.5 * STENCIL[k] * gram[:, 128 * k : 128 * k + 128]
    nonlocal_part = mm(ra[:, :, 0:128].reshape(128, 128), ra[:, :, 128:256].reshape(128, 128), NT)
    gram[:, 0:128] = gram[:, 0:128] + once + once.T + nonlocal_part

    s_copies = []
    for step in range(1, bands):
        peer = band_at(step)
        s_copies.append(send(
            gram.at[pl.ds(pl.multiple_of(peer["band"] * 16, 16), 16), pl.ds(0, 128)], rb.at[band],
            s_send.at[step - 1], s_recv.at[step - 1], peer,
        ))
    rb[band] = gram[pl.ds(pl.multiple_of(band * 16, 16), 16), 0:128]
    finish(3)
    for copy in s_copies:
        copy.wait_recv()
    rd[dom] = jnp.sum(rb[...], axis=0)
    d_copies = [
        send(rd.at[dom], rd.at[dom], s_send.at[bands - 2 + step], s_recv.at[bands - 2 + step], dom_at(step))
        for step in range(1, domains)
    ]
    finish(4)
    for copy in d_copies:
        copy.wait_recv()
    gram_out[...] = jnp.sum(rd[...], axis=0) * (1.0 / (domains * 32768))

    for copy in a_copies + b_copies + f_copies + q_copies + n_copies + s_copies + d_copies:
        copy.wait_send()
    for copies in h_copies:
        for copy in copies:
            copy.wait_send()


def local(domains, bands, orbitals, potential, coupling, projectors, slot_atom, slot_domain_block, slot_count):
    vmem = pl.BlockSpec(memory_space=pltpu.VMEM)
    smem = pl.BlockSpec(memory_space=pltpu.SMEM)
    hbm = pl.BlockSpec(memory_space=pltpu.HBM)
    sums = bands + domains - 2
    return pl.pallas_call(
        functools.partial(kernel, domains, bands),
        out_shape=(
            jax.ShapeDtypeStruct((16, 8, 32, 128), BF16),
            jax.ShapeDtypeStruct((16, 128), F32),
        ),
        in_specs=[hbm, hbm, smem, hbm, hbm, hbm, smem],
        out_specs=(vmem, vmem),
        scratch_shapes=[
            pltpu.VMEM((16, 8, 32, 128), BF16),
            pltpu.VMEM((8, 32, 128), F32),
            pltpu.VMEM((256, 512), BF16),
            pltpu.VMEM((1, 256), jnp.int32),
            pltpu.VMEM((1, 256), jnp.int32),
            pltpu.VMEM((16, 128, 256), BF16),
            pltpu.VMEM((2, 128 + REACH, 16, 128), BF16),
            pltpu.VMEM((8, 2, LANES + REACH, 16, 128), BF16),
            pltpu.VMEM((8, LANES, 16, 128), BF16),
            pltpu.VMEM((4, 16, 32, 128), BF16),
            pltpu.VMEM((4, 16, 32, 128), BF16),
            pltpu.VMEM((16, 8, 32, 128), F32),
            pltpu.VMEM((256, 256), BF16),
            pltpu.VMEM((192, 256), BF16),
            pltpu.VMEM((8, 64, 256), F32),
            pltpu.VMEM((8, 16, 256), F32),
            pltpu.VMEM((8, 16, 256), F32),
            pltpu.VMEM((3, 64, 128), F32),
            pltpu.VMEM((6, 64, 128), F32),
            pltpu.VMEM((256, 256), BF16),
            pltpu.VMEM((256, 512), BF16),
            pltpu.VMEM((256, 128), BF16),
            pltpu.VMEM((256, 128), BF16),
            pltpu.VMEM((128, 256), F32),
            pltpu.VMEM((128, 256), BF16),
            pltpu.VMEM((8, 16, 256), BF16),
            pltpu.VMEM((128, 768), F32),
            pltpu.VMEM((8, 16, 128), F32),
            pltpu.VMEM((domains, 16, 128), F32),
            pltpu.SemaphoreType.DMA((5,)),
            pltpu.SemaphoreType.DMA((7,)),
            pltpu.SemaphoreType.DMA((7,)),
            pltpu.SemaphoreType.DMA((2, 7)),
            pltpu.SemaphoreType.DMA((2, 7)),
            pltpu.SemaphoreType.DMA((8,)),
            pltpu.SemaphoreType.DMA((8,)),
            pltpu.SemaphoreType.DMA((2, 4)),
            pltpu.SemaphoreType.DMA((2, 4)),
            pltpu.SemaphoreType.DMA((4,)),
            pltpu.SemaphoreType.DMA((4,)),
            pltpu.SemaphoreType.DMA((7,)),
            pltpu.SemaphoreType.DMA((7,)),
            pltpu.SemaphoreType.DMA((sums,)),
            pltpu.SemaphoreType.DMA((sums,)),
            pltpu.SemaphoreType.DMA((1,)),
        ],
        compiler_params=pltpu.CompilerParams(
            collective_id=0, has_side_effects=True, vmem_limit_bytes=62 * 1024 * 1024
        ),
    )(
        orbitals, potential, coupling, projectors,
        slot_atom.reshape(1, -1), slot_domain_block.reshape(1, -1), slot_count,
    )


def solution(mesh):
    return jax.shard_map(
        functools.partial(local, mesh.shape["dom"], mesh.shape["band"]),
        mesh=mesh,
        in_specs=(
            P("band", "dom", None, None),
            P("dom", None, None),
            P(),
            P("dom", None),
            P("dom"),
            P("dom"),
            P("dom"),
        ),
        out_specs=(P("band", "dom", None, None), P("band", None)),
        check_vma=False,
    )
```

```python
import functools

import jax
import jax.numpy as jnp
from jax import lax
from jax.experimental import pallas as pl
from jax.experimental.pallas import tpu as pltpu
from jax.sharding import PartitionSpec as P

MESH = pl.DeviceIdType.MESH
F32 = jnp.float32
BF16 = jnp.bfloat16
STENCIL = (-205.0 / 72.0, 8.0 / 5.0, -1.0 / 5.0, 8.0 / 315.0, -1.0 / 560.0)
NN = (((1,), (0,)), ((), ()))
NT = (((1,), (1,)), ((), ()))
LANES = 16
REACH = 4


def mm(a, b, dims=NN):
    return lax.dot_general(a, b, dims, preferred_element_type=F32)


def iota(shape, dim):
    return lax.broadcasted_iota(jnp.int32, shape, dim)


def one(mask):
    return jnp.where(mask, 1.0, 0.0).astype(BF16)


def split(value):
    high = value.astype(BF16)
    return high, (value - high.astype(F32)).astype(BF16)


def plane_matrix():
    r, c = iota((256, 256), 0), iota((256, 256), 1)
    same_plane, same_row = (r >> 5) == (c >> 5), (r & 31) == (c & 31)
    apart, turn = jnp.abs((r >> 5) - (c >> 5)), ((r & 31) - (c & 31)) & 31
    value = jnp.where(r == c, -1.5 * STENCIL[0], 0.0)
    for k in range(1, 5):
        value = jnp.where(same_plane & ((turn == k) | (turn == 32 - k)), -0.5 * STENCIL[k], value)
        value = jnp.where(same_row & (apart == k), -0.5 * STENCIL[k], value)
    return value


def lane_matrix():
    turn = (iota((128, 128), 0) - iota((128, 128), 1)) & 127
    value = jnp.zeros((128, 128), F32)
    for k in range(1, 5):
        value = jnp.where((turn == k) | (turn == 128 - k), -0.5 * STENCIL[k], value)
    return value


def boundary_matrix(parity):
    r, c = iota((128, 128), 0), iota((128, 128), 1)
    apart = ((c >> 5) - (r >> 5)) * (1 - 2 * parity)
    value = jnp.zeros((128, 128), F32)
    for k in range(1, 5):
        value = jnp.where(((r & 31) == (c & 31)) & (apart == 4 - k), -0.5 * STENCIL[k], value)
    return value


def kernel(
    domains, bands,
    v_in, pot_in, coupling, proj_in, atom_in, block_in, count,
    out_hbm, gram_out,
    out, v, pot, proj, atom, block, tv, vt, va, hb, low, high, acc, gt, at, pt, cf, sp, q, rq, pm, lm, zm, mb, pott, p3, ra,
    gram, rb, rd,
    in_sem, a_send, a_recv, b_send, b_recv, f_send, f_recv, h_send, h_recv, q_send, q_recv, n_send, n_recv, s_send, s_recv, own_sem,
):
    dom, band = lax.axis_index("dom"), lax.axis_index("band")

    def dom_at(step):
        return {"dom": lax.rem(dom + step + domains, domains)}

    def band_at(step):
        return {"band": lax.rem(band + step, bands)}

    loads = [
        pltpu.make_async_copy(src, dst, in_sem.at[place])
        for place, (src, dst) in enumerate(
            ((block_in, block), (proj_in, proj), (atom_in, atom), (pot_in, pot))
        )
    ]
    v_loads = [
        pltpu.make_async_copy(v_in.at[pl.ds(4 * part, 4)], v.at[pl.ds(4 * part, 4)], in_sem.at[4 + part])
        for part in range(4)
    ]
    for load in v_loads + loads:
        load.start()

    peers = [band_at(step) for step in range(1, bands)] + [dom_at(step) for step in range(1, domains)]
    barrier = pltpu.get_barrier_semaphore()
    for peer in peers:
        pl.semaphore_signal(barrier, inc=1, device_id=peer, device_id_type=MESH)

    def send(src, dst, send_sem, recv_sem, peer):
        copy = pltpu.make_async_remote_copy(
            src_ref=src, dst_ref=dst, send_sem=send_sem, recv_sem=recv_sem, device_id=peer, device_id_type=MESH
        )
        copy.start()
        return copy

    r, c = iota((256, 256), 0), iota((256, 256), 1)
    pm[...] = one(((r & 15) == (c >> 4)) & ((r >> 4) == (c & 15)))

    small_eye = one(iota((128, 128), 0) == iota((128, 128), 1))

    for part in range(4):
        v_loads[part].wait()
        for o in range(4 * part, 4 * part + 4):
            tv[o] = mm(small_eye, v[o].reshape(256, 128), NT).astype(BF16)

    for share in range(8):
        span = slice(LANES * share, LANES * share + LANES)
        tiles = mm(pm[...], tv[:, span, :].reshape(256, 256)).astype(BF16).reshape(LANES, 16, 256)
        vt[0, span] = tiles[:, :, 0:128]
        vt[1, span] = tiles[:, :, 128:256]
    vt[:, 128 : 128 + REACH] = vt[:, 0:REACH]

    pl.semaphore_wait(barrier, len(peers))

    parity = lax.rem(band, 2)
    a_copies, b_copies = [], []
    for step in range(1, bands):
        peer = band_at(step)
        other, side = peer["band"], lax.rem(peer["band"], 2)
        a_copies.append(send(
            vt.at[side, pl.ds(LANES * other, LANES)], va.at[band, side, pl.ds(0, LANES)],
            a_send.at[step - 1], a_recv.at[step - 1], peer,
        ))
    own = pltpu.make_async_copy(vt.at[:, pl.ds(LANES * band, LANES + REACH)], va.at[band], own_sem.at[0])
    own.start()

    def send_halos(k):
        return (
            send(v.at[:, 8 - k], low.at[4 - k], h_send.at[0, k - 1], h_recv.at[0, k - 1], dom_at(1)),
            send(v.at[:, k - 1], high.at[k - 1], h_send.at[1, k - 1], h_recv.at[1, k - 1], dom_at(-1)),
        )

    h_copies = [send_halos(1), send_halos(2)]
    for step in range(1, bands):
        peer = band_at(step)
        other, side = peer["band"], lax.rem(peer["band"], 2)
        b_copies.append(send(
            vt.at[1 - side, pl.ds(LANES * other, LANES + REACH)], va.at[band, 1 - side],
            b_send.at[0, step - 1], b_recv.at[0, step - 1], peer,
        ))
        b_copies.append(send(
            vt.at[side, pl.ds(LANES * other + LANES, REACH)], va.at[band, side, pl.ds(LANES, REACH)],
            b_send.at[1, step - 1], b_recv.at[1, step - 1], peer,
        ))

    onward = dom_at(2 * parity - 1)

    def forward(source, place):
        return send(va.at[source, parity, pl.ds(0, LANES)], hb.at[source], f_send.at[place], f_recv.at[place], onward)

    for load in loads:
        load.wait()
    half_of = block[...] & 1
    live = iota((1, 256), 1) < count[0]
    gt[...] = one((r == (block[...] >> 1)) & live)
    window = (((atom[...] >> 6) - dom + 1 + domains) & (domains - 1)) * 64 + (atom[...] & 63)
    at[...] = one(iota((192, 256), 0) == window)
    for pair in range(4):
        pt[2 * pair : 2 * pair + 2] = mm(small_eye, proj[:, 128 * pair : 128 * pair + 128], NT).reshape(2, 64, 256)

    @pl.loop(0, 16, step=4)
    def _(first):
        picked = mm(tv[pl.ds(first, 4)].reshape(512, 256), gt[...])
        for i in range(4):
            points = jnp.where(half_of == 0, picked[128 * i : 128 * i + 64], picked[128 * i + 64 : 128 * i + 128])
            for p in range(8):
                cf[p, pl.ds(first + i, 1), :] = jnp.sum(points * pt[p], axis=0, keepdims=True)

    rest = cf[...].reshape(128, 256)
    total = jnp.zeros((192, 128), F32)
    for _ in range(3):
        part = rest.astype(BF16)
        rest = rest - part.astype(F32)
        total = total + mm(at[...], part, NT)
    q[...] = total.reshape(3, 64, 128)
    q_copies = [
        send(q.at[pl.ds(1, 2)], rq.at[pl.ds(1, 2)], q_send.at[0], q_recv.at[0], dom_at(1)),
        send(q.at[pl.ds(0, 2)], rq.at[pl.ds(3, 2)], q_send.at[1], q_recv.at[1], dom_at(-1)),
        send(q.at[2], rq.at[0], q_send.at[2], q_recv.at[2], dom_at(2)),
        send(q.at[0], rq.at[5], q_send.at[3], q_recv.at[3], dom_at(-2)),
    ]

    own.wait()
    f_copies = [forward(band, 0)]
    for step, copy in enumerate(a_copies, 1):
        copy.wait_recv()
        f_copies.append(forward(lax.rem(band - step + bands, bands), step))
    lm[:, 0:256], lm[:, 256:512] = split(plane_matrix())
    zm[0:128], zm[128:256] = split(lane_matrix())

    @pl.loop(0, 16, step=2)
    def _(first):
        values = [v[first + i].reshape(256, 128) for i in range(2)]
        wide = jnp.concatenate(values, axis=1)
        summed = mm(lm[...], jnp.concatenate([wide, wide], axis=0))
        for i in range(2):
            lanes = mm(jnp.concatenate([values[i], values[i]], axis=1), zm[...])
            local_part = summed[:, 128 * i : 128 * i + 128] + lanes + pot[...].reshape(256, 128) * values[i].astype(F32)
            acc[first + i] = local_part.reshape(8, 32, 128)

    rows = []
    for p in range(8):
        line = jnp.zeros((16, 128), F32)
        for j in range(8):
            line = jnp.where((iota((16, 128), 1) >> 4) == j, coupling[p, j], line)
        rows.append(jnp.where((iota((16, 128), 1) & 15) == iota((16, 128), 0), line, 0.0))
    mixing = jnp.concatenate(rows, axis=0)

    for copy in q_copies:
        copy.wait_recv()
    owned = jnp.concatenate([rq[0] + rq[1] + q[0], rq[2] + q[1] + rq[3], q[2] + rq[4] + rq[5]], axis=0)
    coupled = lax.dot_general(mixing, owned, NT, precision=lax.Precision.HIGHEST, preferred_element_type=F32)
    own_rows = owned[64:128]
    p3[:, 0:128] = mm(small_eye, jnp.concatenate(split(own_rows), axis=0), NT).astype(BF16)
    p3[:, 128:256] = lax.dot_general(
        mixing, jnp.concatenate([own_rows, own_rows], axis=0), NT, precision=lax.Precision.HIGHEST, preferred_element_type=F32
    ).astype(BF16)
    n_copies = []
    for step in range(1, bands):
        peer = band_at(step)
        n_copies.append(send(
            p3.at[pl.ds(pl.multiple_of(peer["band"] * 16, 16), 16)], ra.at[band],
            n_send.at[step - 1], n_recv.at[step - 1], peer,
        ))
    ra[band] = p3[pl.ds(pl.multiple_of(band * 16, 16), 16), :]
    sp[...] = mm(coupled.astype(BF16), at[...]).reshape(8, 16, 256)

    gt_twice = jnp.concatenate([gt[...], gt[...]], axis=1)

    @pl.loop(0, 16, step=2)
    def _(first):
        placed = []
        for i in range(2):
            added = pt[0] * sp[0, pl.ds(first + i, 1), :]
            for p in range(1, 8):
                added = added + pt[p] * sp[p, pl.ds(first + i, 1), :]
            placed += [jnp.where(half_of == 0, added, 0.0), jnp.where(half_of == 1, added, 0.0)]
        parts = split(jnp.concatenate(placed, axis=0))
        projected = mm(gt_twice, jnp.concatenate(parts, axis=1), NT)
        for i in range(2):
            acc[first + i] = acc[first + i] + projected[:, 128 * i : 128 * i + 128].reshape(8, 32, 128)


    def finish(k):
        for copy in h_copies[k - 1]:
            copy.wait_recv()
        for side in range(2):
            plane = 3 + k if side else 4 - k
            for half in range(2):
                span = slice(16 * half, 16 * half + 16)
                value = acc[:, plane, span, :]
                for near in range(k):
                    halo = high[near, :, span, :] if side else low[3 - near, :, span, :]
                    reach = 8 + near - plane if side else plane + 1 + near
                    value = value - 0.5 * STENCIL[reach] * halo.astype(F32)
                out[:, plane, span, :] = value.astype(BF16)

    finish(1)
    finish(2)

    pott[...] = pot[...].reshape(256, 128).T
    mb[0:128], mb[128:256] = split(boundary_matrix(parity))
    gram[...] = jnp.zeros_like(gram)
    for copy in b_copies:
        copy.wait_recv()
    h_copies += [send_halos(3), send_halos(4)]

    @pl.loop(0, LANES, step=4)
    def _(first):
        lanes = [
            jnp.concatenate([va[:, 0, first + i].reshape(128, 128), va[:, 1, first + i].reshape(128, 128)], axis=1)
            for i in range(8)
        ]
        images = []
        for i in range(4):
            weights = pott[pl.ds(LANES * band + first + i, 1), :]
            image = mm(jnp.concatenate([lanes[i], lanes[i]], axis=1), lm[...], NT) + weights * lanes[i].astype(F32)
            images.append(image.astype(BF16))
        rows = [jnp.concatenate(images, axis=1)]
        rows += [jnp.concatenate(lanes[k : k + 4], axis=1) for k in range(1, 5)]
        gram[:, 0:640] += mm(jnp.concatenate(lanes[0:4], axis=1), jnp.concatenate(rows, axis=0), NT)

    for copy in f_copies:
        copy.wait_recv()

    @pl.loop(0, LANES, step=4)
    def _(first):
        near, far = [], []
        for i in range(4):
            near.append(va[:, 1 - parity, first + i].reshape(128, 128))
            across = hb[:, first + i].reshape(128, 128)
            far.append(mm(jnp.concatenate([across, across], axis=1), mb[...]).astype(BF16))
        gram[:, 640:768] += mm(jnp.concatenate(near, axis=1), jnp.concatenate(far, axis=1), NT)

    for copy in n_copies:
        copy.wait_recv()
    once = gram[:, 640:768]
    for k in range(1, 5):
        once = once - 0.5 * STENCIL[k] * gram[:, 128 * k : 128 * k + 128]
    nonlocal_part = mm(ra[:, :, 0:128].reshape(128, 128), ra[:, :, 128:256].reshape(128, 128), NT)
    gram[:, 0:128] = gram[:, 0:128] + once + once.T + nonlocal_part

    s_copies = []
    for step in range(1, bands):
        peer = band_at(step)
        s_copies.append(send(
            gram.at[pl.ds(pl.multiple_of(peer["band"] * 16, 16), 16), pl.ds(0, 128)], rb.at[band],
            s_send.at[step - 1], s_recv.at[step - 1], peer,
        ))
    rb[band] = gram[pl.ds(pl.multiple_of(band * 16, 16), 16), 0:128]
    finish(3)
    for copy in s_copies:
        copy.wait_recv()
    rd[dom] = jnp.sum(rb[...], axis=0).astype(BF16)
    d_copies = [
        send(rd.at[dom], rd.at[dom], s_send.at[bands - 2 + step], s_recv.at[bands - 2 + step], dom_at(step))
        for step in range(1, domains)
    ]
    finish(4)
    leave = pltpu.make_async_copy(out, out_hbm, own_sem.at[1])
    leave.start()
    for copy in d_copies:
        copy.wait_recv()
    gram_out[...] = jnp.sum(rd[...].astype(F32), axis=0) * (1.0 / (domains * 32768))

    leave.wait()
    for copy in a_copies + b_copies + f_copies + q_copies + n_copies + s_copies + d_copies:
        copy.wait_send()
    for copies in h_copies:
        for copy in copies:
            copy.wait_send()


PARTS = 4


def place(applied, gram, applied_out, gram_out, held, held_gram, come, go):
    refs = [
        (applied.at[pl.ds(16 // PARTS * part, 16 // PARTS)], held.at[pl.ds(16 // PARTS * part, 16 // PARTS)],
         applied_out.at[pl.ds(16 // PARTS * part, 16 // PARTS)])
        for part in range(PARTS)
    ]
    refs.append((gram, held_gram, gram_out))
    arriving = [pltpu.make_async_copy(src, held_part, come.at[i]) for i, (src, held_part, _) in enumerate(refs)]
    leaving = [pltpu.make_async_copy(held_part, dst, go.at[i]) for i, (_, held_part, dst) in enumerate(refs)]
    for copy in arriving:
        copy.start()
    for first, second in zip(arriving, leaving):
        first.wait()
        second.start()
    for copy in leaving:
        copy.wait()


def local(domains, bands, orbitals, potential, coupling, projectors, slot_atom, slot_domain_block, slot_count):
    vmem = pl.BlockSpec(memory_space=pltpu.VMEM)
    smem = pl.BlockSpec(memory_space=pltpu.SMEM)
    hbm = pl.BlockSpec(memory_space=pltpu.HBM)
    sums = bands + domains - 2
    shapes = (jax.ShapeDtypeStruct((16, 8, 32, 128), BF16), jax.ShapeDtypeStruct((16, 128), F32))
    results = pl.pallas_call(
        functools.partial(kernel, domains, bands),
        out_shape=shapes,
        in_specs=[hbm, hbm, smem, hbm, hbm, hbm, smem],
        out_specs=(hbm, vmem),
        scratch_shapes=[
            pltpu.VMEM((16, 8, 32, 128), BF16),
            pltpu.VMEM((16, 8, 32, 128), BF16),
            pltpu.VMEM((8, 32, 128), F32),
            pltpu.VMEM((256, 512), BF16),
            pltpu.VMEM((1, 256), jnp.int32),
            pltpu.VMEM((1, 256), jnp.int32),
            pltpu.VMEM((16, 128, 256), BF16),
            pltpu.VMEM((2, 128 + REACH, 16, 128), BF16),
            pltpu.VMEM((8, 2, LANES + REACH, 16, 128), BF16),
            pltpu.VMEM((8, LANES, 16, 128), BF16),
            pltpu.VMEM((4, 16, 32, 128), BF16),
            pltpu.VMEM((4, 16, 32, 128), BF16),
            pltpu.VMEM((16, 8, 32, 128), F32),
            pltpu.VMEM((256, 256), BF16),
            pltpu.VMEM((192, 256), BF16),
            pltpu.VMEM((8, 64, 256), F32),
            pltpu.VMEM((8, 16, 256), F32),
            pltpu.VMEM((8, 16, 256), F32),
            pltpu.VMEM((3, 64, 128), F32),
            pltpu.VMEM((6, 64, 128), F32),
            pltpu.VMEM((256, 256), BF16),
            pltpu.VMEM((256, 512), BF16),
            pltpu.VMEM((256, 128), BF16),
            pltpu.VMEM((256, 128), BF16),
            pltpu.VMEM((128, 256), F32),
            pltpu.VMEM((128, 256), BF16),
            pltpu.VMEM((8, 16, 256), BF16),
            pltpu.VMEM((128, 768), F32),
            pltpu.VMEM((8, 16, 128), F32),
            pltpu.VMEM((domains, 16, 128), BF16),
            pltpu.SemaphoreType.DMA((8,)),
            pltpu.SemaphoreType.DMA((7,)),
            pltpu.SemaphoreType.DMA((7,)),
            pltpu.SemaphoreType.DMA((2, 7)),
            pltpu.SemaphoreType.DMA((2, 7)),
            pltpu.SemaphoreType.DMA((8,)),
            pltpu.SemaphoreType.DMA((8,)),
            pltpu.SemaphoreType.DMA((2, 4)),
            pltpu.SemaphoreType.DMA((2, 4)),
            pltpu.SemaphoreType.DMA((4,)),
            pltpu.SemaphoreType.DMA((4,)),
            pltpu.SemaphoreType.DMA((7,)),
            pltpu.SemaphoreType.DMA((7,)),
            pltpu.SemaphoreType.DMA((sums,)),
            pltpu.SemaphoreType.DMA((sums,)),
            pltpu.SemaphoreType.DMA((2,)),
        ],
        compiler_params=pltpu.CompilerParams(
            collective_id=0, has_side_effects=True, vmem_limit_bytes=62 * 1024 * 1024
        ),
    )(
        orbitals, potential, coupling, projectors,
        slot_atom.reshape(1, -1), slot_domain_block.reshape(1, -1), slot_count,
    )
    return pl.pallas_call(
        place,
        out_shape=shapes,
        in_specs=[hbm, hbm],
        out_specs=(hbm, hbm),
        scratch_shapes=[
            pltpu.VMEM((16, 8, 32, 128), BF16),
            pltpu.VMEM((16, 128), F32),
            pltpu.SemaphoreType.DMA((PARTS + 1,)),
            pltpu.SemaphoreType.DMA((PARTS + 1,)),
        ],
        compiler_params=pltpu.CompilerParams(vmem_limit_bytes=62 * 1024 * 1024),
    )(*results)


def solution(mesh):
    return jax.shard_map(
        functools.partial(local, mesh.shape["dom"], mesh.shape["band"]),
        mesh=mesh,
        in_specs=(
            P("band", "dom", None, None),
            P("dom", None, None),
            P(),
            P("dom", None),
            P("dom"),
            P("dom"),
            P("dom"),
        ),
        out_specs=(P("band", "dom", None, None), P("band", None)),
        check_vma=False,
    )
```

```python
import functools

import jax
import jax.numpy as jnp
from jax import lax
from jax.experimental import pallas as pl
from jax.experimental.pallas import tpu as pltpu
from jax.sharding import PartitionSpec as P

MESH = pl.DeviceIdType.MESH
F32 = jnp.float32
BF16 = jnp.bfloat16
STENCIL = (-205.0 / 72.0, 8.0 / 5.0, -1.0 / 5.0, 8.0 / 315.0, -1.0 / 560.0)
NN = (((1,), (0,)), ((), ()))
NT = (((1,), (1,)), ((), ()))
LANES = 32
HALF = 16
REACH = 4


def mm(a, b, dims=NN):
    return lax.dot_general(a, b, dims, preferred_element_type=F32)


def iota(shape, dim):
    return lax.broadcasted_iota(jnp.int32, shape, dim)


def one(mask):
    return jnp.where(mask, 1.0, 0.0).astype(BF16)


def split(value):
    high = value.astype(BF16)
    return high, (value - high.astype(F32)).astype(BF16)


def plane_matrix():
    r, c = iota((256, 256), 0), iota((256, 256), 1)
    same_plane, same_row = (r >> 5) == (c >> 5), (r & 31) == (c & 31)
    apart, turn = jnp.abs((r >> 5) - (c >> 5)), ((r & 31) - (c & 31)) & 31
    value = jnp.where(r == c, -1.5 * STENCIL[0], 0.0)
    for k in range(1, 5):
        value = jnp.where(same_plane & ((turn == k) | (turn == 32 - k)), -0.5 * STENCIL[k], value)
        value = jnp.where(same_row & (apart == k), -0.5 * STENCIL[k], value)
    return value


def lane_matrix():
    turn = (iota((128, 128), 0) - iota((128, 128), 1)) & 127
    value = jnp.zeros((128, 128), F32)
    for k in range(1, 5):
        value = jnp.where((turn == k) | (turn == 128 - k), -0.5 * STENCIL[k], value)
    return value


def boundary_matrix(parity):
    r, c = iota((128, 128), 0), iota((128, 128), 1)
    apart = ((c >> 5) - (r >> 5)) * (1 - 2 * parity)
    value = jnp.zeros((128, 128), F32)
    for k in range(1, 5):
        value = jnp.where(((r & 31) == (c & 31)) & (apart == 4 - k), -0.5 * STENCIL[k], value)
    return value


def kernel(
    domains, bands,
    v_in, pot_in, coupling, proj_in, atom_in, block_in, count,
    out, gram_out,
    v, pot, proj, atom, block, tv, vt, va, hb, hc, low, high, acc, gt, at, pt, cf, sp, q, rq, pm, lm, zm, mb, pott, p3, ra,
    gram, rb, rd,
    in_sem, a_send, a_recv, b_send, b_recv, f_send, f_recv, h_send, h_recv, q_send, q_recv, n_send, n_recv, s_send, s_recv, own_sem,
):
    dom, band = lax.axis_index("dom"), lax.axis_index("band")

    def dom_at(step):
        return {"dom": lax.rem(dom + step + domains, domains)}

    def band_at(step):
        return {"band": lax.rem(band + step, bands)}

    loads = [
        pltpu.make_async_copy(src, dst, in_sem.at[place])
        for place, (src, dst) in enumerate(
            ((block_in, block), (proj_in, proj), (atom_in, atom), (pot_in, pot))
        )
    ]
    v_loads = [
        pltpu.make_async_copy(v_in.at[pl.ds(4 * part, 4)], v.at[pl.ds(4 * part, 4)], in_sem.at[4 + part])
        for part in range(4)
    ]
    for load in v_loads + loads:
        load.start()

    parity = lax.rem(band, 2)
    chip = band - parity
    across = {"band": band + 1 - 2 * parity}
    onward = {"dom": lax.rem(dom + 2 * parity - 1 + domains, domains), "band": band + 1 - 2 * parity}
    peers = [onward] + [band_at(step) for step in range(1, bands)] + [dom_at(step) for step in range(1, domains)]
    barrier = pltpu.get_barrier_semaphore()
    for peer in peers:
        pl.semaphore_signal(barrier, inc=1, device_id=peer, device_id_type=MESH)

    def send(src, dst, send_sem, recv_sem, peer):
        copy = pltpu.make_async_remote_copy(
            src_ref=src, dst_ref=dst, send_sem=send_sem, recv_sem=recv_sem, device_id=peer, device_id_type=MESH
        )
        copy.start()
        return copy

    r, c = iota((256, 256), 0), iota((256, 256), 1)
    pm[...] = one(((r & 15) == (c >> 4)) & ((r >> 4) == (c & 15)))

    small_eye = one(iota((128, 128), 0) == iota((128, 128), 1))

    for part in range(4):
        v_loads[part].wait()
        for o in range(4 * part, 4 * part + 4):
            tv[o] = mm(small_eye, v[o].reshape(256, 128), NT).astype(BF16)

    for share in range(8):
        span = slice(HALF * share, HALF * share + HALF)
        tiles = mm(pm[...], tv[:, span, :].reshape(256, 256)).astype(BF16).reshape(HALF, 16, 256)
        vt[0, span] = tiles[:, :, 0:128]
        vt[1, span] = tiles[:, :, 128:256]
    vt[:, 128 : 128 + REACH] = vt[:, 0:REACH]

    pl.semaphore_wait(barrier, len(peers))

    a_copies, b_copies = [], []
    for step in range(1, bands):
        peer = band_at(step)
        other, side = peer["band"], lax.rem(peer["band"], 2)
        start = HALF * (other - side)
        a_copies.append(send(
            vt.at[side, pl.ds(start + HALF * side, HALF)], va.at[band, pl.ds(HALF * side, HALF)],
            a_send.at[step - 1], a_recv.at[step - 1], peer,
        ))
    own = pltpu.make_async_copy(vt.at[parity, pl.ds(HALF * chip, LANES + REACH)], va.at[band], own_sem.at[0])
    own.start()

    def send_halos(k):
        return (
            send(v.at[:, 8 - k], low.at[4 - k], h_send.at[0, k - 1], h_recv.at[0, k - 1], dom_at(1)),
            send(v.at[:, k - 1], high.at[k - 1], h_send.at[1, k - 1], h_recv.at[1, k - 1], dom_at(-1)),
        )

    h_copies = [send_halos(1), send_halos(2)]
    def forward(source, place):
        half = va.at[source, pl.ds(HALF * parity, HALF)]
        return (
            send(half, hb.at[source], f_send.at[0, place], f_recv.at[0, place], onward),
            send(half, hc.at[source], f_send.at[1, place], f_recv.at[1, place], across),
        )

    for load in loads:
        load.wait()
    half_of = block[...] & 1
    live = iota((1, 256), 1) < count[0]
    gt[...] = one((r == (block[...] >> 1)) & live)
    window = (((atom[...] >> 6) - dom + 1 + domains) & (domains - 1)) * 64 + (atom[...] & 63)
    at[...] = one(iota((192, 256), 0) == window)
    for pair in range(4):
        pt[2 * pair : 2 * pair + 2] = mm(small_eye, proj[:, 128 * pair : 128 * pair + 128], NT).reshape(2, 64, 256)

    @pl.loop(0, 16, step=4)
    def _(first):
        picked = mm(tv[pl.ds(first, 4)].reshape(512, 256), gt[...])
        for i in range(4):
            points = jnp.where(half_of == 0, picked[128 * i : 128 * i + 64], picked[128 * i + 64 : 128 * i + 128])
            for p in range(8):
                cf[p, pl.ds(first + i, 1), :] = jnp.sum(points * pt[p], axis=0, keepdims=True)

    rest = cf[...].reshape(128, 256)
    total = jnp.zeros((192, 128), F32)
    for _ in range(3):
        part = rest.astype(BF16)
        rest = rest - part.astype(F32)
        total = total + mm(at[...], part, NT)
    q[...] = total.reshape(3, 64, 128)
    q_copies = [
        send(q.at[pl.ds(1, 2)], rq.at[pl.ds(1, 2)], q_send.at[0], q_recv.at[0], dom_at(1)),
        send(q.at[pl.ds(0, 2)], rq.at[pl.ds(3, 2)], q_send.at[1], q_recv.at[1], dom_at(-1)),
        send(q.at[2], rq.at[0], q_send.at[2], q_recv.at[2], dom_at(2)),
        send(q.at[0], rq.at[5], q_send.at[3], q_recv.at[3], dom_at(-2)),
    ]

    for step in range(1, bands):
        peer = band_at(step)
        other, side = peer["band"], lax.rem(peer["band"], 2)
        start = HALF * (other - side)
        b_copies.append(send(
            vt.at[side, pl.ds(start + HALF * (1 - side), HALF)], va.at[band, pl.ds(HALF * (1 - side), HALF)],
            b_send.at[0, step - 1], b_recv.at[0, step - 1], peer,
        ))
        b_copies.append(send(
            vt.at[side, pl.ds(start + LANES, REACH)], va.at[band, pl.ds(LANES, REACH)],
            b_send.at[1, step - 1], b_recv.at[1, step - 1], peer,
        ))

    own.wait()
    f_copies = [*forward(band, 0)]
    for step, copy in enumerate(a_copies, 1):
        copy.wait_recv()
        f_copies += forward(lax.rem(band - step + bands, bands), step)
    lm[:, 0:256], lm[:, 256:512] = split(plane_matrix())
    zm[0:128], zm[128:256] = split(lane_matrix())

    @pl.loop(0, 16, step=2)
    def _(first):
        values = [v[first + i].reshape(256, 128) for i in range(2)]
        wide = jnp.concatenate(values, axis=1)
        summed = mm(lm[...], jnp.concatenate([wide, wide], axis=0))
        for i in range(2):
            lanes = mm(jnp.concatenate([values[i], values[i]], axis=1), zm[...])
            local_part = summed[:, 128 * i : 128 * i + 128] + lanes + pot[...].reshape(256, 128) * values[i].astype(F32)
            acc[first + i] = local_part.reshape(8, 32, 128)

    rows = []
    for p in range(8):
        line = jnp.zeros((16, 128), F32)
        for j in range(8):
            line = jnp.where((iota((16, 128), 1) >> 4) == j, coupling[p, j], line)
        rows.append(jnp.where((iota((16, 128), 1) & 15) == iota((16, 128), 0), line, 0.0))
    mixing = jnp.concatenate(rows, axis=0)

    for copy in q_copies:
        copy.wait_recv()
    owned = jnp.concatenate([rq[0] + rq[1] + q[0], rq[2] + q[1] + rq[3], q[2] + rq[4] + rq[5]], axis=0)
    coupled = lax.dot_general(mixing, owned, NT, precision=lax.Precision.HIGHEST, preferred_element_type=F32)
    own_rows = owned[64:128]
    p3[:, 0:128] = mm(small_eye, jnp.concatenate(split(own_rows), axis=0), NT).astype(BF16)
    p3[:, 128:256] = lax.dot_general(
        mixing, jnp.concatenate([own_rows, own_rows], axis=0), NT, precision=lax.Precision.HIGHEST, preferred_element_type=F32
    ).astype(BF16)
    n_copies = []
    for step in range(1, bands):
        peer = band_at(step)
        n_copies.append(send(
            p3.at[pl.ds(pl.multiple_of(peer["band"] * 16, 16), 16)], ra.at[band],
            n_send.at[step - 1], n_recv.at[step - 1], peer,
        ))
    ra[band] = p3[pl.ds(pl.multiple_of(band * 16, 16), 16), :]
    sp[...] = mm(coupled.astype(BF16), at[...]).reshape(8, 16, 256)

    gt_twice = jnp.concatenate([gt[...], gt[...]], axis=1)

    @pl.loop(0, 16, step=2)
    def _(first):
        placed = []
        for i in range(2):
            added = pt[0] * sp[0, pl.ds(first + i, 1), :]
            for p in range(1, 8):
                added = added + pt[p] * sp[p, pl.ds(first + i, 1), :]
            placed += [jnp.where(half_of == 0, added, 0.0), jnp.where(half_of == 1, added, 0.0)]
        parts = split(jnp.concatenate(placed, axis=0))
        projected = mm(gt_twice, jnp.concatenate(parts, axis=1), NT)
        for i in range(2):
            acc[first + i] = acc[first + i] + projected[:, 128 * i : 128 * i + 128].reshape(8, 32, 128)


    def finish(k):
        for copy in h_copies[k - 1]:
            copy.wait_recv()
        for side in range(2):
            plane = 3 + k if side else 4 - k
            for half in range(2):
                span = slice(16 * half, 16 * half + 16)
                value = acc[:, plane, span, :]
                for near in range(k):
                    halo = high[near, :, span, :] if side else low[3 - near, :, span, :]
                    reach = 8 + near - plane if side else plane + 1 + near
                    value = value - 0.5 * STENCIL[reach] * halo.astype(F32)
                out[:, plane, span, :] = value.astype(BF16)

    finish(1)
    finish(2)

    for group in range(2):
        pott[group] = pot[4 * group : 4 * group + 4].reshape(128, 128).T
    for place, side in ((0, 1 - parity), (256, parity)):
        mb[place : place + 128], mb[place + 128 : place + 256] = split(boundary_matrix(side))
    few_planes = jnp.concatenate([lm[0:128, 0:128], lm[0:128, 256:384]], axis=1)
    for copy in n_copies:
        copy.wait_recv()
    gram[:, 0:128] = mm(ra[:, :, 0:128].reshape(128, 128), ra[:, :, 128:256].reshape(128, 128), NT)
    gram[:, 128:768] = jnp.zeros((128, 640), F32)

    def within(first):
        lanes = [va[:, first + i].reshape(128, 128) for i in range(12)]
        images = []
        for i in range(8):
            weights = pott[parity, pl.ds(HALF * chip + first + i, 1), :]
            image = mm(jnp.concatenate([lanes[i], lanes[i]], axis=1), few_planes, NT) + weights * lanes[i].astype(F32)
            images.append(image.astype(BF16))
        rows = [jnp.concatenate(images, axis=1)]
        rows += [jnp.concatenate(lanes[k : k + 8], axis=1) for k in range(1, 5)]
        gram[:, 0:640] += mm(jnp.concatenate(lanes[0:8], axis=1), jnp.concatenate(rows, axis=0), NT)

    within(HALF * parity)
    for copy in b_copies:
        copy.wait_recv()
    h_copies += [send_halos(3), send_halos(4)]
    for first in (HALF * parity + 8, HALF * (1 - parity), HALF * (1 - parity) + 8):
        within(first)
    for copy in f_copies:
        copy.wait_recv()

    @pl.loop(0, HALF, step=8)
    def _(first):
        near, far = [], []
        for i in range(8):
            near.append(va[:, HALF * (1 - parity) + first + i].reshape(128, 128))
            beyond, beside = hb[:, first + i].reshape(128, 128), hc[:, first + i].reshape(128, 128)
            far.append(mm(jnp.concatenate([beyond, beyond, beside, beside], axis=1), mb[...]).astype(BF16))
        gram[:, 640:768] += mm(jnp.concatenate(near, axis=1), jnp.concatenate(far, axis=1), NT)

    once = gram[:, 640:768]
    for k in range(1, 5):
        once = once - 0.5 * STENCIL[k] * gram[:, 128 * k : 128 * k + 128]
    gram[:, 0:128] = gram[:, 0:128] + once + once.T

    s_copies = []
    for step in range(1, bands):
        peer = band_at(step)
        s_copies.append(send(
            gram.at[pl.ds(pl.multiple_of(peer["band"] * 16, 16), 16), pl.ds(0, 128)], rb.at[band],
            s_send.at[step - 1], s_recv.at[step - 1], peer,
        ))
    rb[band] = gram[pl.ds(pl.multiple_of(band * 16, 16), 16), 0:128]
    finish(3)
    for copy in s_copies:
        copy.wait_recv()
    rd[dom] = jnp.sum(rb[...], axis=0).astype(BF16)
    d_copies = [
        send(rd.at[dom], rd.at[dom], s_send.at[bands - 2 + step], s_recv.at[bands - 2 + step], dom_at(step))
        for step in range(1, domains)
    ]
    finish(4)
    for copy in d_copies:
        copy.wait_recv()
    gram_out[...] = jnp.sum(rd[...].astype(F32), axis=0) * (1.0 / (domains * 32768))

    for copy in a_copies + b_copies + f_copies + q_copies + n_copies + s_copies + d_copies:
        copy.wait_send()
    for copies in h_copies:
        for copy in copies:
            copy.wait_send()


def local(domains, bands, orbitals, potential, coupling, projectors, slot_atom, slot_domain_block, slot_count):
    vmem = pl.BlockSpec(memory_space=pltpu.VMEM)
    smem = pl.BlockSpec(memory_space=pltpu.SMEM)
    hbm = pl.BlockSpec(memory_space=pltpu.HBM)
    sums = bands + domains - 2
    return pl.pallas_call(
        functools.partial(kernel, domains, bands),
        out_shape=(pltpu.VMEM((16, 8, 32, 128), BF16), pltpu.VMEM((16, 128), F32)),
        in_specs=[hbm, hbm, smem, hbm, hbm, hbm, smem],
        out_specs=(vmem, vmem),
        scratch_shapes=[
            pltpu.VMEM((16, 8, 32, 128), BF16),
            pltpu.VMEM((8, 32, 128), F32),
            pltpu.VMEM((256, 512), BF16),
            pltpu.VMEM((1, 256), jnp.int32),
            pltpu.VMEM((1, 256), jnp.int32),
            pltpu.VMEM((16, 128, 256), BF16),
            pltpu.VMEM((2, 128 + REACH, 16, 128), BF16),
            pltpu.VMEM((8, LANES + REACH, 16, 128), BF16),
            pltpu.VMEM((8, HALF, 16, 128), BF16),
            pltpu.VMEM((8, HALF, 16, 128), BF16),
            pltpu.VMEM((4, 16, 32, 128), BF16),
            pltpu.VMEM((4, 16, 32, 128), BF16),
            pltpu.VMEM((16, 8, 32, 128), F32),
            pltpu.VMEM((256, 256), BF16),
            pltpu.VMEM((192, 256), BF16),
            pltpu.VMEM((8, 64, 256), F32),
            pltpu.VMEM((8, 16, 256), F32),
            pltpu.VMEM((8, 16, 256), F32),
            pltpu.VMEM((3, 64, 128), F32),
            pltpu.VMEM((6, 64, 128), F32),
            pltpu.VMEM((256, 256), BF16),
            pltpu.VMEM((256, 512), BF16),
            pltpu.VMEM((256, 128), BF16),
            pltpu.VMEM((512, 128), BF16),
            pltpu.VMEM((2, 128, 128), F32),
            pltpu.VMEM((128, 256), BF16),
            pltpu.VMEM((8, 16, 256), BF16),
            pltpu.VMEM((128, 768), F32),
            pltpu.VMEM((8, 16, 128), F32),
            pltpu.VMEM((domains, 16, 128), BF16),
            pltpu.SemaphoreType.DMA((8,)),
            pltpu.SemaphoreType.DMA((7,)),
            pltpu.SemaphoreType.DMA((7,)),
            pltpu.SemaphoreType.DMA((2, 7)),
            pltpu.SemaphoreType.DMA((2, 7)),
            pltpu.SemaphoreType.DMA((2, 8)),
            pltpu.SemaphoreType.DMA((2, 8)),
            pltpu.SemaphoreType.DMA((2, 4)),
            pltpu.SemaphoreType.DMA((2, 4)),
            pltpu.SemaphoreType.DMA((4,)),
            pltpu.SemaphoreType.DMA((4,)),
            pltpu.SemaphoreType.DMA((7,)),
            pltpu.SemaphoreType.DMA((7,)),
            pltpu.SemaphoreType.DMA((sums,)),
            pltpu.SemaphoreType.DMA((sums,)),
            pltpu.SemaphoreType.DMA((2,)),
        ],
        compiler_params=pltpu.CompilerParams(
            collective_id=0, has_side_effects=True, vmem_limit_bytes=62 * 1024 * 1024
        ),
    )(
        orbitals, potential, coupling, projectors,
        slot_atom.reshape(1, -1), slot_domain_block.reshape(1, -1), slot_count,
    )


def solution(mesh):
    return jax.shard_map(
        functools.partial(local, mesh.shape["dom"], mesh.shape["band"]),
        mesh=mesh,
        in_specs=(
            P("band", "dom", None, None),
            P("dom", None, None),
            P(),
            P("dom", None),
            P("dom"),
            P("dom"),
            P("dom"),
        ),
        out_specs=(P("band", "dom", None, None), P("band", None)),
        check_vma=False,
    )
```

```python
import functools

import jax
import jax.numpy as jnp
from jax import lax
from jax.experimental import pallas as pl
from jax.experimental.pallas import tpu as pltpu
from jax.sharding import PartitionSpec as P

MESH = pl.DeviceIdType.MESH
F32 = jnp.float32
BF16 = jnp.bfloat16
STENCIL = (-205.0 / 72.0, 8.0 / 5.0, -1.0 / 5.0, 8.0 / 315.0, -1.0 / 560.0)
NN = (((1,), (0,)), ((), ()))
NT = (((1,), (1,)), ((), ()))
LANES = 32
HALF = 16
REACH = 4


def mm(a, b, dims=NN):
    return lax.dot_general(a, b, dims, preferred_element_type=F32)


def iota(shape, dim):
    return lax.broadcasted_iota(jnp.int32, shape, dim)


def one(mask):
    return jnp.where(mask, 1.0, 0.0).astype(BF16)


def split(value):
    high = value.astype(BF16)
    return high, (value - high.astype(F32)).astype(BF16)


def plane_matrix():
    r, c = iota((256, 256), 0), iota((256, 256), 1)
    same_plane, same_row = (r >> 5) == (c >> 5), (r & 31) == (c & 31)
    apart, turn = jnp.abs((r >> 5) - (c >> 5)), ((r & 31) - (c & 31)) & 31
    value = jnp.where(r == c, -1.5 * STENCIL[0], 0.0)
    for k in range(1, 5):
        value = jnp.where(same_plane & ((turn == k) | (turn == 32 - k)), -0.5 * STENCIL[k], value)
        value = jnp.where(same_row & (apart == k), -0.5 * STENCIL[k], value)
    return value


def lane_matrix():
    turn = (iota((128, 128), 0) - iota((128, 128), 1)) & 127
    value = jnp.zeros((128, 128), F32)
    for k in range(1, 5):
        value = jnp.where((turn == k) | (turn == 128 - k), -0.5 * STENCIL[k], value)
    return value


def boundary_matrix(parity):
    r, c = iota((128, 128), 0), iota((128, 128), 1)
    apart = ((c >> 5) - (r >> 5)) * (1 - 2 * parity)
    value = jnp.zeros((128, 128), F32)
    for k in range(1, 5):
        value = jnp.where(((r & 31) == (c & 31)) & (apart == 4 - k), -0.5 * STENCIL[k], value)
    return value


def kernel(
    domains, bands,
    v_in, pot_in, coupling, proj_in, atom_in, block_in, count,
    out, gram_out,
    v, pot, proj, atom, block, tv, vt, va, hb, hc, low, high, acc, gt, at, pt, cf, sp, q, rq, pm, lm, zm, mb, pott, p3, ra,
    gram, rb, rd,
    in_sem, a_send, a_recv, b_send, b_recv, f_send, f_recv, h_send, h_recv, q_send, q_recv, n_send, n_recv, s_send, s_recv, own_sem,
):
    dom, band = lax.axis_index("dom"), lax.axis_index("band")

    def dom_at(step):
        return {"dom": lax.rem(dom + step + domains, domains)}

    def band_at(step):
        return {"band": lax.rem(band + step, bands)}

    loads = [
        pltpu.make_async_copy(src, dst, in_sem.at[place])
        for place, (src, dst) in enumerate(
            ((block_in, block), (proj_in, proj), (atom_in, atom), (pot_in, pot))
        )
    ]
    v_loads = [
        pltpu.make_async_copy(v_in.at[pl.ds(4 * part, 4)], v.at[pl.ds(4 * part, 4)], in_sem.at[4 + part])
        for part in range(4)
    ]
    for load in v_loads + loads:
        load.start()

    parity = lax.rem(band, 2)
    chip = band - parity
    across = {"band": band + 1 - 2 * parity}
    onward = {"dom": lax.rem(dom + 2 * parity - 1 + domains, domains), "band": band + 1 - 2 * parity}
    peers = [onward] + [band_at(step) for step in range(1, bands)] + [dom_at(step) for step in range(1, domains)]
    barrier = pltpu.get_barrier_semaphore()
    for peer in peers:
        pl.semaphore_signal(barrier, inc=1, device_id=peer, device_id_type=MESH)

    def send(src, dst, send_sem, recv_sem, peer):
        copy = pltpu.make_async_remote_copy(
            src_ref=src, dst_ref=dst, send_sem=send_sem, recv_sem=recv_sem, device_id=peer, device_id_type=MESH
        )
        copy.start()
        return copy

    r, c = iota((256, 256), 0), iota((256, 256), 1)
    pm[...] = one(((r & 15) == (c >> 4)) & ((r >> 4) == (c & 15)))

    small_eye = one(iota((128, 128), 0) == iota((128, 128), 1))

    for part in range(4):
        v_loads[part].wait()
        for o in range(4 * part, 4 * part + 4):
            tv[o] = mm(small_eye, v[o].reshape(256, 128), NT).astype(BF16)

    for share in range(8):
        span = slice(HALF * share, HALF * share + HALF)
        tiles = mm(pm[...], tv[:, span, :].reshape(256, 256)).astype(BF16).reshape(HALF, 16, 256)
        vt[0, span] = tiles[:, :, 0:128]
        vt[1, span] = tiles[:, :, 128:256]
    vt[:, 128 : 128 + REACH] = vt[:, 0:REACH]

    pl.semaphore_wait(barrier, len(peers))

    a_copies, b_copies = [], []
    for step in range(1, bands):
        peer = band_at(step)
        other, side = peer["band"], lax.rem(peer["band"], 2)
        start = HALF * (other - side)
        a_copies.append(send(
            vt.at[side, pl.ds(start + HALF * side, HALF)], va.at[band, pl.ds(HALF * side, HALF)],
            a_send.at[step - 1], a_recv.at[step - 1], peer,
        ))
    own = pltpu.make_async_copy(vt.at[parity, pl.ds(HALF * chip, LANES + REACH)], va.at[band], own_sem.at[0])
    own.start()

    def send_halos(k):
        return (
            send(v.at[:, 8 - k], low.at[4 - k], h_send.at[0, k - 1], h_recv.at[0, k - 1], dom_at(1)),
            send(v.at[:, k - 1], high.at[k - 1], h_send.at[1, k - 1], h_recv.at[1, k - 1], dom_at(-1)),
        )

    h_copies = [send_halos(1), send_halos(2)]
    def forward(source, place):
        half = va.at[source, pl.ds(HALF * parity, HALF)]
        return (
            send(half, hb.at[source], f_send.at[0, place], f_recv.at[0, place], onward),
            send(half, hc.at[source], f_send.at[1, place], f_recv.at[1, place], across),
        )

    for load in loads:
        load.wait()
    half_of = block[...] & 1
    live = iota((1, 256), 1) < count[0]
    gt[...] = one((r == (block[...] >> 1)) & live)
    window = (((atom[...] >> 6) - dom + 1 + domains) & (domains - 1)) * 64 + (atom[...] & 63)
    at[...] = one(iota((192, 256), 0) == window)
    for pair in range(4):
        pt[2 * pair : 2 * pair + 2] = mm(small_eye, proj[:, 128 * pair : 128 * pair + 128], NT).reshape(2, 64, 256)

    @pl.loop(0, 16, step=4)
    def _(first):
        picked = mm(tv[pl.ds(first, 4)].reshape(512, 256), gt[...])
        for i in range(4):
            points = jnp.where(half_of == 0, picked[128 * i : 128 * i + 64], picked[128 * i + 64 : 128 * i + 128])
            for p in range(8):
                cf[p, pl.ds(first + i, 1), :] = jnp.sum(points * pt[p], axis=0, keepdims=True)

    rest = cf[...].reshape(128, 256)
    total = jnp.zeros((192, 128), F32)
    for _ in range(3):
        part = rest.astype(BF16)
        rest = rest - part.astype(F32)
        total = total + mm(at[...], part, NT)
    q[...] = total.reshape(3, 64, 128)
    q_copies = [
        send(q.at[pl.ds(1, 2)], rq.at[pl.ds(1, 2)], q_send.at[0], q_recv.at[0], dom_at(1)),
        send(q.at[pl.ds(0, 2)], rq.at[pl.ds(3, 2)], q_send.at[1], q_recv.at[1], dom_at(-1)),
        send(q.at[2], rq.at[0], q_send.at[2], q_recv.at[2], dom_at(2)),
        send(q.at[0], rq.at[5], q_send.at[3], q_recv.at[3], dom_at(-2)),
    ]

    for step in range(1, bands):
        peer = band_at(step)
        other, side = peer["band"], lax.rem(peer["band"], 2)
        start = HALF * (other - side)
        b_copies.append(send(
            vt.at[side, pl.ds(start + HALF * (1 - side), HALF)], va.at[band, pl.ds(HALF * (1 - side), HALF)],
            b_send.at[0, step - 1], b_recv.at[0, step - 1], peer,
        ))
        b_copies.append(send(
            vt.at[side, pl.ds(start + LANES, REACH)], va.at[band, pl.ds(LANES, REACH)],
            b_send.at[1, step - 1], b_recv.at[1, step - 1], peer,
        ))

    own.wait()
    f_copies = [*forward(band, 0)]
    for step, copy in enumerate(a_copies, 1):
        copy.wait_recv()
        f_copies += forward(lax.rem(band - step + bands, bands), step)
    lm[:, 0:256], lm[:, 256:512] = split(plane_matrix())
    zm[0:128], zm[128:256] = split(lane_matrix())

    @pl.loop(0, 16, step=2)
    def _(first):
        values = [v[first + i].reshape(256, 128) for i in range(2)]
        wide = jnp.concatenate(values, axis=1)
        summed = mm(lm[...], jnp.concatenate([wide, wide], axis=0))
        for i in range(2):
            lanes = mm(jnp.concatenate([values[i], values[i]], axis=1), zm[...])
            local_part = summed[:, 128 * i : 128 * i + 128] + lanes + pot[...].reshape(256, 128) * values[i].astype(F32)
            acc[first + i] = local_part.reshape(8, 32, 128)

    rows = []
    for p in range(8):
        line = jnp.zeros((16, 128), F32)
        for j in range(8):
            line = jnp.where((iota((16, 128), 1) >> 4) == j, coupling[p, j], line)
        rows.append(jnp.where((iota((16, 128), 1) & 15) == iota((16, 128), 0), line, 0.0))
    mixing = jnp.concatenate(rows, axis=0)

    for copy in q_copies:
        copy.wait_recv()
    owned = jnp.concatenate([rq[0] + rq[1] + q[0], rq[2] + q[1] + rq[3], q[2] + rq[4] + rq[5]], axis=0)
    coupled = lax.dot_general(mixing, owned, NT, precision=lax.Precision.HIGHEST, preferred_element_type=F32)
    own_rows = owned[64:128]
    p3[:, 0:128] = mm(small_eye, jnp.concatenate(split(own_rows), axis=0), NT).astype(BF16)
    p3[:, 128:256] = lax.dot_general(
        mixing, jnp.concatenate([own_rows, own_rows], axis=0), NT, precision=lax.Precision.HIGHEST, preferred_element_type=F32
    ).astype(BF16)
    n_copies = []
    for step in range(1, bands):
        peer = band_at(step)
        n_copies.append(send(
            p3.at[pl.ds(pl.multiple_of(peer["band"] * 16, 16), 16)], ra.at[band],
            n_send.at[step - 1], n_recv.at[step - 1], peer,
        ))
    ra[band] = p3[pl.ds(pl.multiple_of(band * 16, 16), 16), :]
    sp[...] = mm(coupled.astype(BF16), at[...]).reshape(8, 16, 256)

    gt_twice = jnp.concatenate([gt[...], gt[...]], axis=1)

    @pl.loop(0, 16, step=2)
    def _(first):
        placed = []
        for i in range(2):
            added = pt[0] * sp[0, pl.ds(first + i, 1), :]
            for p in range(1, 8):
                added = added + pt[p] * sp[p, pl.ds(first + i, 1), :]
            placed += [jnp.where(half_of == 0, added, 0.0), jnp.where(half_of == 1, added, 0.0)]
        parts = split(jnp.concatenate(placed, axis=0))
        projected = mm(gt_twice, jnp.concatenate(parts, axis=1), NT)
        for i in range(2):
            acc[first + i] = acc[first + i] + projected[:, 128 * i : 128 * i + 128].reshape(8, 32, 128)


    def finish(k):
        for copy in h_copies[k - 1]:
            copy.wait_recv()
        for side in range(2):
            plane = 3 + k if side else 4 - k
            for half in range(2):
                span = slice(16 * half, 16 * half + 16)
                value = acc[:, plane, span, :]
                for near in range(k):
                    halo = high[near, :, span, :] if side else low[3 - near, :, span, :]
                    reach = 8 + near - plane if side else plane + 1 + near
                    value = value - 0.5 * STENCIL[reach] * halo.astype(F32)
                out[:, plane, span, :] = value.astype(BF16)

    finish(1)
    finish(2)

    for group in range(2):
        pott[group] = pot[4 * group : 4 * group + 4].reshape(128, 128).T
    for place, side in ((0, 1 - parity), (256, parity)):
        mb[place : place + 128], mb[place + 128 : place + 256] = split(boundary_matrix(side))
    few_planes = jnp.concatenate([lm[0:128, 0:128], lm[0:128, 256:384]], axis=1)
    for copy in n_copies:
        copy.wait_recv()
    gram[:, 0:128] = mm(ra[:, :, 0:128].reshape(128, 128), ra[:, :, 128:256].reshape(128, 128), NT)
    gram[:, 128:768] = jnp.zeros((128, 640), F32)

    def within(first):
        lanes = [va[:, first + i].reshape(128, 128) for i in range(12)]
        images = []
        for i in range(8):
            weights = pott[parity, pl.ds(HALF * chip + first + i, 1), :]
            image = mm(jnp.concatenate([lanes[i], lanes[i]], axis=1), few_planes, NT) + weights * lanes[i].astype(F32)
            images.append(image.astype(BF16))
        rows = [jnp.concatenate(images, axis=1)]
        rows += [jnp.concatenate(lanes[k : k + 8], axis=1) for k in range(1, 5)]
        gram[:, 0:640] += mm(jnp.concatenate(lanes[0:8], axis=1), jnp.concatenate(rows, axis=0), NT)

    within(HALF * parity)
    for copy in b_copies:
        copy.wait_recv()
    h_copies += [send_halos(3), send_halos(4)]
    for first in (HALF * parity + 8, HALF * (1 - parity), HALF * (1 - parity) + 8):
        within(first)
    for copy in f_copies:
        copy.wait_recv()

    @pl.loop(0, HALF, step=8)
    def _(first):
        near, far = [], []
        for i in range(8):
            near.append(va[:, HALF * (1 - parity) + first + i].reshape(128, 128))
            beyond, beside = hb[:, first + i].reshape(128, 128), hc[:, first + i].reshape(128, 128)
            far.append(mm(jnp.concatenate([beyond, beyond, beside, beside], axis=1), mb[...]).astype(BF16))
        gram[:, 640:768] += mm(jnp.concatenate(near, axis=1), jnp.concatenate(far, axis=1), NT)

    once = gram[:, 640:768]
    for k in range(1, 5):
        once = once - 0.5 * STENCIL[k] * gram[:, 128 * k : 128 * k + 128]
    gram[:, 0:128] = gram[:, 0:128] + once + once.T

    s_copies = []
    for step in range(1, bands):
        peer = band_at(step)
        s_copies.append(send(
            gram.at[pl.ds(pl.multiple_of(peer["band"] * 16, 16), 16), pl.ds(0, 128)], rb.at[band],
            s_send.at[step - 1], s_recv.at[step - 1], peer,
        ))
    rb[band] = gram[pl.ds(pl.multiple_of(band * 16, 16), 16), 0:128]
    for copy in s_copies:
        copy.wait_recv()
    rd[dom] = jnp.sum(rb[...], axis=0).astype(BF16)
    for step in range(1, domains):
        send(rd.at[dom], rd.at[dom], s_send.at[bands - 1], s_recv.at[bands - 1], dom_at(step))
    finish(3)
    finish(4)
    for copy in a_copies + b_copies + f_copies + q_copies + n_copies + s_copies:
        copy.wait_send()
    for copies in h_copies:
        for copy in copies:
            copy.wait_send()
    others = rd.at[pl.ds(0, domains - 1)]
    every = pltpu.make_async_remote_copy(
        src_ref=others, dst_ref=others, send_sem=s_send.at[bands - 1], recv_sem=s_recv.at[bands - 1],
        device_id=dom_at(1), device_id_type=MESH,
    )
    every.wait_recv()
    gram_out[...] = jnp.sum(rd[...].astype(F32), axis=0) * (1.0 / (domains * 32768))

    every.wait_send()


def local(domains, bands, orbitals, potential, coupling, projectors, slot_atom, slot_domain_block, slot_count):
    vmem = pl.BlockSpec(memory_space=pltpu.VMEM)
    smem = pl.BlockSpec(memory_space=pltpu.SMEM)
    hbm = pl.BlockSpec(memory_space=pltpu.HBM)
    sums = bands
    return pl.pallas_call(
        functools.partial(kernel, domains, bands),
        out_shape=(pltpu.VMEM((16, 8, 32, 128), BF16), pltpu.VMEM((16, 128), F32)),
        in_specs=[hbm, hbm, smem, hbm, hbm, hbm, smem],
        out_specs=(vmem, vmem),
        scratch_shapes=[
            pltpu.VMEM((16, 8, 32, 128), BF16),
            pltpu.VMEM((8, 32, 128), F32),
            pltpu.VMEM((256, 512), BF16),
            pltpu.VMEM((1, 256), jnp.int32),
            pltpu.VMEM((1, 256), jnp.int32),
            pltpu.VMEM((16, 128, 256), BF16),
            pltpu.VMEM((2, 128 + REACH, 16, 128), BF16),
            pltpu.VMEM((8, LANES + REACH, 16, 128), BF16),
            pltpu.VMEM((8, HALF, 16, 128), BF16),
            pltpu.VMEM((8, HALF, 16, 128), BF16),
            pltpu.VMEM((4, 16, 32, 128), BF16),
            pltpu.VMEM((4, 16, 32, 128), BF16),
            pltpu.VMEM((16, 8, 32, 128), F32),
            pltpu.VMEM((256, 256), BF16),
            pltpu.VMEM((192, 256), BF16),
            pltpu.VMEM((8, 64, 256), F32),
            pltpu.VMEM((8, 16, 256), F32),
            pltpu.VMEM((8, 16, 256), F32),
            pltpu.VMEM((3, 64, 128), F32),
            pltpu.VMEM((6, 64, 128), F32),
            pltpu.VMEM((256, 256), BF16),
            pltpu.VMEM((256, 512), BF16),
            pltpu.VMEM((256, 128), BF16),
            pltpu.VMEM((512, 128), BF16),
            pltpu.VMEM((2, 128, 128), F32),
            pltpu.VMEM((128, 256), BF16),
            pltpu.VMEM((8, 16, 256), BF16),
            pltpu.VMEM((128, 768), F32),
            pltpu.VMEM((8, 16, 128), F32),
            pltpu.VMEM((domains, 16, 128), BF16),
            pltpu.SemaphoreType.DMA((8,)),
            pltpu.SemaphoreType.DMA((7,)),
            pltpu.SemaphoreType.DMA((7,)),
            pltpu.SemaphoreType.DMA((2, 7)),
            pltpu.SemaphoreType.DMA((2, 7)),
            pltpu.SemaphoreType.DMA((2, 8)),
            pltpu.SemaphoreType.DMA((2, 8)),
            pltpu.SemaphoreType.DMA((2, 4)),
            pltpu.SemaphoreType.DMA((2, 4)),
            pltpu.SemaphoreType.DMA((4,)),
            pltpu.SemaphoreType.DMA((4,)),
            pltpu.SemaphoreType.DMA((7,)),
            pltpu.SemaphoreType.DMA((7,)),
            pltpu.SemaphoreType.DMA((sums,)),
            pltpu.SemaphoreType.DMA((sums,)),
            pltpu.SemaphoreType.DMA((2,)),
        ],
        compiler_params=pltpu.CompilerParams(
            collective_id=0, has_side_effects=True, vmem_limit_bytes=62 * 1024 * 1024
        ),
    )(
        orbitals, potential, coupling, projectors,
        slot_atom.reshape(1, -1), slot_domain_block.reshape(1, -1), slot_count,
    )


def solution(mesh):
    return jax.shard_map(
        functools.partial(local, mesh.shape["dom"], mesh.shape["band"]),
        mesh=mesh,
        in_specs=(
            P("band", "dom", None, None),
            P("dom", None, None),
            P(),
            P("dom", None),
            P("dom"),
            P("dom"),
            P("dom"),
        ),
        out_specs=(P("band", "dom", None, None), P("band", None)),
        check_vma=False,
    )
```

```python
import functools

import jax
import jax.numpy as jnp
from jax import lax
from jax.experimental import pallas as pl
from jax.experimental.pallas import tpu as pltpu
from jax.sharding import PartitionSpec as P

MESH = pl.DeviceIdType.MESH
F32 = jnp.float32
BF16 = jnp.bfloat16
STENCIL = (-205.0 / 72.0, 8.0 / 5.0, -1.0 / 5.0, 8.0 / 315.0, -1.0 / 560.0)
NN = (((1,), (0,)), ((), ()))
NT = (((1,), (1,)), ((), ()))
LANES = 32
HALF = 16
REACH = 4


def mm(a, b, dims=NN):
    return lax.dot_general(a, b, dims, preferred_element_type=F32)


def iota(shape, dim):
    return lax.broadcasted_iota(jnp.int32, shape, dim)


def one(mask):
    return jnp.where(mask, 1.0, 0.0).astype(BF16)


def split(value):
    high = value.astype(BF16)
    return high, (value - high.astype(F32)).astype(BF16)


def plane_matrix():
    r, c = iota((256, 256), 0), iota((256, 256), 1)
    same_plane, same_row = (r >> 5) == (c >> 5), (r & 31) == (c & 31)
    apart, turn = jnp.abs((r >> 5) - (c >> 5)), ((r & 31) - (c & 31)) & 31
    value = jnp.where(r == c, -1.5 * STENCIL[0], 0.0)
    for k in range(1, 5):
        value = jnp.where(same_plane & ((turn == k) | (turn == 32 - k)), -0.5 * STENCIL[k], value)
        value = jnp.where(same_row & (apart == k), -0.5 * STENCIL[k], value)
    return value


def lane_matrix():
    turn = (iota((128, 128), 0) - iota((128, 128), 1)) & 127
    value = jnp.zeros((128, 128), F32)
    for k in range(1, 5):
        value = jnp.where((turn == k) | (turn == 128 - k), -0.5 * STENCIL[k], value)
    return value


def boundary_matrix(parity):
    r, c = iota((128, 128), 0), iota((128, 128), 1)
    apart = ((c >> 5) - (r >> 5)) * (1 - 2 * parity)
    value = jnp.zeros((128, 128), F32)
    for k in range(1, 5):
        value = jnp.where(((r & 31) == (c & 31)) & (apart == 4 - k), -0.5 * STENCIL[k], value)
    return value


def kernel(
    domains, bands,
    v_in, pot_in, coupling, proj_in, atom_in, block_in, count,
    out, gram_out,
    v, pot, proj, atom, block, tv, vt, va, hb, hc, low, high, acc, gt, at, pt, cf, sp, q, rq, pm, lm, zm, mb, pott, p3, ra,
    gram, rb, rd,
    in_sem, a_send, a_recv, b_send, b_recv, f_send, f_recv, h_send, h_recv, q_send, q_recv, n_send, n_recv, s_send, s_recv, own_sem,
):
    dom, band = lax.axis_index("dom"), lax.axis_index("band")

    def dom_at(step):
        return {"dom": lax.rem(dom + step + domains, domains)}

    def band_at(step):
        return {"band": lax.rem(band + step, bands)}

    loads = [
        pltpu.make_async_copy(src, dst, in_sem.at[place])
        for place, (src, dst) in enumerate(
            ((block_in, block), (proj_in, proj), (atom_in, atom), (pot_in, pot))
        )
    ]
    v_loads = [
        pltpu.make_async_copy(v_in.at[pl.ds(4 * part, 4)], v.at[pl.ds(4 * part, 4)], in_sem.at[4 + part])
        for part in range(4)
    ]
    for load in v_loads + loads:
        load.start()

    parity = lax.rem(band, 2)
    chip = band - parity
    across = {"band": band + 1 - 2 * parity}
    onward = {"dom": lax.rem(dom + 2 * parity - 1 + domains, domains), "band": band + 1 - 2 * parity}
    peers = [onward] + [band_at(step) for step in range(1, bands)] + [dom_at(step) for step in range(1, domains)]
    barrier = pltpu.get_barrier_semaphore()
    for peer in peers:
        pl.semaphore_signal(barrier, inc=1, device_id=peer, device_id_type=MESH)

    def send(src, dst, send_sem, recv_sem, peer):
        copy = pltpu.make_async_remote_copy(
            src_ref=src, dst_ref=dst, send_sem=send_sem, recv_sem=recv_sem, device_id=peer, device_id_type=MESH
        )
        copy.start()
        return copy

    r, c = iota((256, 256), 0), iota((256, 256), 1)
    pm[...] = one(((r & 15) == (c >> 4)) & ((r >> 4) == (c & 15)))

    small_eye = one(iota((128, 128), 0) == iota((128, 128), 1))

    for part in range(4):
        v_loads[part].wait()
        for o in range(4 * part, 4 * part + 4):
            tv[o] = mm(small_eye, v[o].reshape(256, 128), NT).astype(BF16)

    for share in range(8):
        span = slice(HALF * share, HALF * share + HALF)
        tiles = mm(pm[...], tv[:, span, :].reshape(256, 256)).astype(BF16).reshape(HALF, 16, 256)
        vt[0, span] = tiles[:, :, 0:128]
        vt[1, span] = tiles[:, :, 128:256]
    vt[:, 128 : 128 + REACH] = vt[:, 0:REACH]

    pl.semaphore_wait(barrier, len(peers))

    a_copies, b_copies = [], []
    for step in range(1, bands):
        peer = band_at(step)
        other, side = peer["band"], lax.rem(peer["band"], 2)
        start = HALF * (other - side)
        a_copies.append(send(
            vt.at[side, pl.ds(start + HALF * side, HALF)], va.at[band, pl.ds(HALF * side, HALF)],
            a_send.at[step - 1], a_recv.at[step - 1], peer,
        ))
    own = pltpu.make_async_copy(vt.at[parity, pl.ds(HALF * chip, LANES + REACH)], va.at[band], own_sem.at[0])
    own.start()

    def together(refs, send_sem, recv_sem):
        return pltpu.make_async_remote_copy(
            src_ref=refs, dst_ref=refs, send_sem=send_sem, recv_sem=recv_sem, device_id=dom_at(1), device_id_type=MESH
        )

    def send_halos(k):
        return (
            send(v.at[:, 8 - k], low.at[4 - k], h_send.at[0, k - 1], h_recv.at[0, k - 1], dom_at(1)),
            send(v.at[:, k - 1], high.at[k - 1], h_send.at[1, k - 1], h_recv.at[1, k - 1], dom_at(-1)),
        )

    h_copies = [send_halos(1), send_halos(2)]
    def forward(source, place):
        half = va.at[source, pl.ds(HALF * parity, HALF)]
        return (
            send(half, hb.at[source], f_send.at[0, place], f_recv.at[0, place], onward),
            send(half, hc.at[source], f_send.at[1, place], f_recv.at[1, place], across),
        )

    for load in loads:
        load.wait()
    half_of = block[...] & 1
    live = iota((1, 256), 1) < count[0]
    gt[...] = one((r == (block[...] >> 1)) & live)
    window = (((atom[...] >> 6) - dom + 1 + domains) & (domains - 1)) * 64 + (atom[...] & 63)
    at[...] = one(iota((192, 256), 0) == window)
    for pair in range(4):
        pt[2 * pair : 2 * pair + 2] = mm(small_eye, proj[:, 128 * pair : 128 * pair + 128], NT).reshape(2, 64, 256)

    @pl.loop(0, 16, step=4)
    def _(first):
        picked = mm(tv[pl.ds(first, 4)].reshape(512, 256), gt[...])
        for i in range(4):
            points = jnp.where(half_of == 0, picked[128 * i : 128 * i + 64], picked[128 * i + 64 : 128 * i + 128])
            for p in range(8):
                cf[p, pl.ds(first + i, 1), :] = jnp.sum(points * pt[p], axis=0, keepdims=True)

    rest = cf[...].reshape(128, 256)
    total = jnp.zeros((192, 128), F32)
    for _ in range(3):
        part = rest.astype(BF16)
        rest = rest - part.astype(F32)
        total = total + mm(at[...], part, NT)
    q[...] = total.reshape(3, 64, 128)
    q_copies = [
        send(q.at[pl.ds(1, 2)], rq.at[pl.ds(1, 2)], q_send.at[0], q_recv.at[0], dom_at(1)),
        send(q.at[pl.ds(0, 2)], rq.at[pl.ds(3, 2)], q_send.at[1], q_recv.at[1], dom_at(-1)),
        send(q.at[2], rq.at[0], q_send.at[2], q_recv.at[2], dom_at(2)),
        send(q.at[0], rq.at[5], q_send.at[3], q_recv.at[3], dom_at(-2)),
    ]

    for step in range(1, bands):
        peer = band_at(step)
        other, side = peer["band"], lax.rem(peer["band"], 2)
        start = HALF * (other - side)
        b_copies.append(send(
            vt.at[side, pl.ds(start + HALF * (1 - side), HALF)], va.at[band, pl.ds(HALF * (1 - side), HALF)],
            b_send.at[0], b_recv.at[0], peer,
        ))
        b_copies.append(send(
            vt.at[side, pl.ds(start + LANES, REACH)], va.at[band, pl.ds(LANES, REACH)],
            b_send.at[1], b_recv.at[1], peer,
        ))

    own.wait()
    f_copies = [*forward(band, 0)]
    for step, copy in enumerate(a_copies, 1):
        copy.wait_recv()
        f_copies += forward(lax.rem(band - step + bands, bands), step)
    lm[:, 0:256], lm[:, 256:512] = split(plane_matrix())
    zm[0:128], zm[128:256] = split(lane_matrix())

    @pl.loop(0, 16, step=2)
    def _(first):
        values = [v[first + i].reshape(256, 128) for i in range(2)]
        wide = jnp.concatenate(values, axis=1)
        summed = mm(lm[...], jnp.concatenate([wide, wide], axis=0))
        for i in range(2):
            lanes = mm(jnp.concatenate([values[i], values[i]], axis=1), zm[...])
            local_part = summed[:, 128 * i : 128 * i + 128] + lanes + pot[...].reshape(256, 128) * values[i].astype(F32)
            acc[first + i] = local_part.reshape(8, 32, 128)

    rows = []
    for p in range(8):
        line = jnp.zeros((16, 128), F32)
        for j in range(8):
            line = jnp.where((iota((16, 128), 1) >> 4) == j, coupling[p, j], line)
        rows.append(jnp.where((iota((16, 128), 1) & 15) == iota((16, 128), 0), line, 0.0))
    mixing = jnp.concatenate(rows, axis=0)

    for copy in q_copies:
        copy.wait_recv()
    owned = jnp.concatenate([rq[0] + rq[1] + q[0], rq[2] + q[1] + rq[3], q[2] + rq[4] + rq[5]], axis=0)
    coupled = lax.dot_general(mixing, owned, NT, precision=lax.Precision.HIGHEST, preferred_element_type=F32)
    own_rows = owned[64:128]
    p3[:, 0:128] = mm(small_eye, jnp.concatenate(split(own_rows), axis=0), NT).astype(BF16)
    p3[:, 128:256] = lax.dot_general(
        mixing, jnp.concatenate([own_rows, own_rows], axis=0), NT, precision=lax.Precision.HIGHEST, preferred_element_type=F32
    ).astype(BF16)
    n_copies = []
    for step in range(1, bands):
        peer = band_at(step)
        n_copies.append(send(
            p3.at[pl.ds(pl.multiple_of(peer["band"] * 16, 16), 16)], ra.at[band],
            n_send.at[step - 1], n_recv.at[step - 1], peer,
        ))
    ra[band] = p3[pl.ds(pl.multiple_of(band * 16, 16), 16), :]
    sp[...] = mm(coupled.astype(BF16), at[...]).reshape(8, 16, 256)

    gt_twice = jnp.concatenate([gt[...], gt[...]], axis=1)

    @pl.loop(0, 16, step=2)
    def _(first):
        placed = []
        for i in range(2):
            added = pt[0] * sp[0, pl.ds(first + i, 1), :]
            for p in range(1, 8):
                added = added + pt[p] * sp[p, pl.ds(first + i, 1), :]
            placed += [jnp.where(half_of == 0, added, 0.0), jnp.where(half_of == 1, added, 0.0)]
        parts = split(jnp.concatenate(placed, axis=0))
        projected = mm(gt_twice, jnp.concatenate(parts, axis=1), NT)
        for i in range(2):
            acc[first + i] = acc[first + i] + projected[:, 128 * i : 128 * i + 128].reshape(8, 32, 128)


    def finish(k):
        for copy in h_copies[k - 1]:
            copy.wait_recv()
        for side in range(2):
            plane = 3 + k if side else 4 - k
            for half in range(2):
                span = slice(16 * half, 16 * half + 16)
                value = acc[:, plane, span, :]
                for near in range(k):
                    halo = high[near, :, span, :] if side else low[3 - near, :, span, :]
                    reach = 8 + near - plane if side else plane + 1 + near
                    value = value - 0.5 * STENCIL[reach] * halo.astype(F32)
                out[:, plane, span, :] = value.astype(BF16)

    finish(1)
    finish(2)

    for group in range(2):
        pott[group] = pot[4 * group : 4 * group + 4].reshape(128, 128).T
    for place, side in ((0, 1 - parity), (256, parity)):
        mb[place : place + 128], mb[place + 128 : place + 256] = split(boundary_matrix(side))
    few_planes = jnp.concatenate([lm[0:128, 0:128], lm[0:128, 256:384]], axis=1)
    for copy in n_copies:
        copy.wait_recv()
    gram[:, 0:128] = mm(ra[:, :, 0:128].reshape(128, 128), ra[:, :, 128:256].reshape(128, 128), NT)
    gram[:, 128:768] = jnp.zeros((128, 640), F32)

    def within(first):
        lanes = [va[:, first + i].reshape(128, 128) for i in range(12)]
        images = []
        for i in range(8):
            weights = pott[parity, pl.ds(HALF * chip + first + i, 1), :]
            image = mm(jnp.concatenate([lanes[i], lanes[i]], axis=1), few_planes, NT) + weights * lanes[i].astype(F32)
            images.append(image.astype(BF16))
        rows = [jnp.concatenate(images, axis=1)]
        rows += [jnp.concatenate(lanes[k : k + 8], axis=1) for k in range(1, 5)]
        gram[:, 0:640] += mm(jnp.concatenate(lanes[0:8], axis=1), jnp.concatenate(rows, axis=0), NT)

    within(HALF * parity)
    b_copies = [
        together(va.at[pl.ds(0, bands - 1), pl.ds(0, HALF)], b_send.at[0], b_recv.at[0]),
        together(va.at[pl.ds(0, bands - 1), pl.ds(LANES, REACH)], b_send.at[1], b_recv.at[1]),
    ]
    for copy in b_copies:
        copy.wait_recv()
    h_copies += [send_halos(3), send_halos(4)]
    for first in (HALF * parity + 8, HALF * (1 - parity), HALF * (1 - parity) + 8):
        within(first)
    for copy in f_copies:
        copy.wait_recv()

    @pl.loop(0, HALF, step=8)
    def _(first):
        near, far = [], []
        for i in range(8):
            near.append(va[:, HALF * (1 - parity) + first + i].reshape(128, 128))
            beyond, beside = hb[:, first + i].reshape(128, 128), hc[:, first + i].reshape(128, 128)
            far.append(mm(jnp.concatenate([beyond, beyond, beside, beside], axis=1), mb[...]).astype(BF16))
        gram[:, 640:768] += mm(jnp.concatenate(near, axis=1), jnp.concatenate(far, axis=1), NT)

    once = gram[:, 640:768]
    for k in range(1, 5):
        once = once - 0.5 * STENCIL[k] * gram[:, 128 * k : 128 * k + 128]
    gram[:, 0:128] = gram[:, 0:128] + once + once.T

    s_copies = []
    for step in range(1, bands):
        peer = band_at(step)
        s_copies.append(send(
            gram.at[pl.ds(pl.multiple_of(peer["band"] * 16, 16), 16), pl.ds(0, 128)], rb.at[band],
            s_send.at[0], s_recv.at[0], peer,
        ))
    rb[band] = gram[pl.ds(pl.multiple_of(band * 16, 16), 16), 0:128]
    s_copies = [together(rb.at[pl.ds(0, bands - 1)], s_send.at[0], s_recv.at[0])]
    s_copies[0].wait_recv()
    rd[dom] = jnp.sum(rb[...], axis=0).astype(BF16)
    for step in range(1, domains):
        send(rd.at[dom], rd.at[dom], s_send.at[1], s_recv.at[1], dom_at(step))
    finish(3)
    finish(4)
    for copy in a_copies + b_copies + f_copies + q_copies + n_copies + s_copies:
        copy.wait_send()
    for copies in h_copies:
        for copy in copies:
            copy.wait_send()
    others = rd.at[pl.ds(0, domains - 1)]
    every = pltpu.make_async_remote_copy(
        src_ref=others, dst_ref=others, send_sem=s_send.at[1], recv_sem=s_recv.at[1],
        device_id=dom_at(1), device_id_type=MESH,
    )
    every.wait_recv()
    gram_out[...] = jnp.sum(rd[...].astype(F32), axis=0) * (1.0 / (domains * 32768))

    every.wait_send()


def local(domains, bands, orbitals, potential, coupling, projectors, slot_atom, slot_domain_block, slot_count):
    vmem = pl.BlockSpec(memory_space=pltpu.VMEM)
    smem = pl.BlockSpec(memory_space=pltpu.SMEM)
    hbm = pl.BlockSpec(memory_space=pltpu.HBM)
    sums = 2
    return pl.pallas_call(
        functools.partial(kernel, domains, bands),
        out_shape=(pltpu.VMEM((16, 8, 32, 128), BF16), pltpu.VMEM((16, 128), F32)),
        in_specs=[hbm, hbm, smem, hbm, hbm, hbm, smem],
        out_specs=(vmem, vmem),
        scratch_shapes=[
            pltpu.VMEM((16, 8, 32, 128), BF16),
            pltpu.VMEM((8, 32, 128), F32),
            pltpu.VMEM((256, 512), BF16),
            pltpu.VMEM((1, 256), jnp.int32),
            pltpu.VMEM((1, 256), jnp.int32),
            pltpu.VMEM((16, 128, 256), BF16),
            pltpu.VMEM((2, 128 + REACH, 16, 128), BF16),
            pltpu.VMEM((8, LANES + REACH, 16, 128), BF16),
            pltpu.VMEM((8, HALF, 16, 128), BF16),
            pltpu.VMEM((8, HALF, 16, 128), BF16),
            pltpu.VMEM((4, 16, 32, 128), BF16),
            pltpu.VMEM((4, 16, 32, 128), BF16),
            pltpu.VMEM((16, 8, 32, 128), F32),
            pltpu.VMEM((256, 256), BF16),
            pltpu.VMEM((192, 256), BF16),
            pltpu.VMEM((8, 64, 256), F32),
            pltpu.VMEM((8, 16, 256), F32),
            pltpu.VMEM((8, 16, 256), F32),
            pltpu.VMEM((3, 64, 128), F32),
            pltpu.VMEM((6, 64, 128), F32),
            pltpu.VMEM((256, 256), BF16),
            pltpu.VMEM((256, 512), BF16),
            pltpu.VMEM((256, 128), BF16),
            pltpu.VMEM((512, 128), BF16),
            pltpu.VMEM((2, 128, 128), F32),
            pltpu.VMEM((128, 256), BF16),
            pltpu.VMEM((8, 16, 256), BF16),
            pltpu.VMEM((128, 768), F32),
            pltpu.VMEM((8, 16, 128), F32),
            pltpu.VMEM((domains, 16, 128), BF16),
            pltpu.SemaphoreType.DMA((8,)),
            pltpu.SemaphoreType.DMA((7,)),
            pltpu.SemaphoreType.DMA((7,)),
            pltpu.SemaphoreType.DMA((2,)),
            pltpu.SemaphoreType.DMA((2,)),
            pltpu.SemaphoreType.DMA((2, 8)),
            pltpu.SemaphoreType.DMA((2, 8)),
            pltpu.SemaphoreType.DMA((2, 4)),
            pltpu.SemaphoreType.DMA((2, 4)),
            pltpu.SemaphoreType.DMA((4,)),
            pltpu.SemaphoreType.DMA((4,)),
            pltpu.SemaphoreType.DMA((7,)),
            pltpu.SemaphoreType.DMA((7,)),
            pltpu.SemaphoreType.DMA((sums,)),
            pltpu.SemaphoreType.DMA((sums,)),
            pltpu.SemaphoreType.DMA((2,)),
        ],
        compiler_params=pltpu.CompilerParams(
            collective_id=0, has_side_effects=True, vmem_limit_bytes=62 * 1024 * 1024
        ),
    )(
        orbitals, potential, coupling, projectors,
        slot_atom.reshape(1, -1), slot_domain_block.reshape(1, -1), slot_count,
    )


def solution(mesh):
    return jax.shard_map(
        functools.partial(local, mesh.shape["dom"], mesh.shape["band"]),
        mesh=mesh,
        in_specs=(
            P("band", "dom", None, None),
            P("dom", None, None),
            P(),
            P("dom", None),
            P("dom"),
            P("dom"),
            P("dom"),
        ),
        out_specs=(P("band", "dom", None, None), P("band", None)),
        check_vma=False,
    )
```
